256 devices in a mesh: lat: 16 (over x_lo, y, core), lon: 16 (over x_hi, z).
Axes of the slice: x: 4 (x_hi: 2, x_lo: 2; x = x_hi * 2 + x_lo), y: 4, z: 8, core: 2. Of those that a mesh axis runs over, the one named last changes fastest.
Arguments:
- inputs: bfloat16 [128, 1024, 256], P('lat', 'lon'), may hold values from -44 to 44, as said below
- cotangent: bfloat16 [128, 1024, 256], P('lat', 'lon'), may hold values from -6 to 6
- valid_cells: int32 [128, 1024], replicated, may hold values from 0 to 1, as said below
- gain_one: float32 [256], replicated, may hold values from 0.1 to 1.9
- shift_one: float32 [256], replicated, may hold values from -2 to 2
- gain_two: float32 [256], replicated, may hold values from 0.1 to 1.9
- shift_two: float32 [256], replicated, may hold values from -2 to 2
- qkv_weight: bfloat16 [256, 768], replicated, may hold values from -0.375 to 0.375
- proj_weight: bfloat16 [256, 256], replicated, may hold values from -0.375 to 0.375
- up_weight: bfloat16 [256, 1024], replicated, may hold values from -0.375 to 0.375
- down_weight: bfloat16 [1024, 256], replicated, may hold values from -0.1875 to 0.1875
- bias_table: float32 [8, 225], replicated, may hold values from -4 to 300
Outputs:
- output: bfloat16 [128, 1024, 256], P('lat', 'lon')
- grad_inputs: bfloat16 [128, 1024, 256], P('lat', 'lon')
- grad_qkv: float32 [256, 768], replicated
- grad_proj: float32 [256, 256], replicated
- grad_up: float32 [256, 1024], replicated
- grad_down: float32 [1024, 256], replicated
- grad_gain_one: float32 [256], replicated
- grad_shift_one: float32 [256], replicated
- grad_gain_two: float32 [256], replicated
- grad_shift_two: float32 [256], replicated
- grad_table: float32 [8, 225], replicated
The draws below stay inside these ranges and needn't reach their ends.
Inputs may be any that keep to these rules, and one draw needn't show every extreme that they name: `inputs`: each entry is a scaled patch feature. `valid_cells`: 0 marks land or padding; rows from 112 on and columns from 900 on are padding.
All inputs are finite; a program needn't handle non-finite values.
Results may differ from the reference program's by a relative error of at most 0.017.
Values may be sent and summed in bfloat16 or wider, within the bound.
No kernel may reach another device: no remote copies, remote signals or barrier semaphores. Data moves between devices by JAX's collectives and lax.ppermute only.
A program may use at most 64 MiB of HBM per device.

```python
import math
import jax
import jax.numpy as jnp
from jax import lax

CH = 256
HEADS = 8
MLP = 1024
WIN = 8
HEAD_DIM = 32
NLAT = 128
NLON = 1024
TOKENS = 131072


def draw_inputs(key, part):
    key = jax.random.fold_in(key, 1)
    row_key, chan_key, noise_key = jax.random.split(key, 3)
    row_scale = jnp.exp(jax.random.uniform(row_key, (NLAT, NLON, 1), jnp.float32, -1.2, 1.2))
    chan_scale = jnp.exp(jax.random.uniform(chan_key, (CH,), jnp.float32, -1.2, 1.2))
    noise = jnp.clip(jax.random.normal(noise_key, (NLAT, NLON, CH), jnp.float32), -4.0, 4.0)
    values = noise * row_scale * chan_scale
    return values.astype(jnp.bfloat16)


def draw_valid_cells(key, part):
    key = jax.random.fold_in(key, 3)
    sea_cells = jax.random.randint(key, (NLAT, NLON), 0, 10) >= 3
    row_pos = jnp.arange(NLAT, dtype=jnp.int32)[:, None]
    col_pos = jnp.arange(NLON, dtype=jnp.int32)[None, :]
    inside = (row_pos < NLAT * 225 // 256) & (col_pos < NLON * 225 // 256)
    return (sea_cells & inside).astype(jnp.int32)


def draw_bias_table(key, part):
    key = jax.random.fold_in(key, 2)
    entries = (2 * WIN - 1) * (2 * WIN - 1)
    table_base = jax.random.uniform(key, (HEADS, entries), jnp.float32, -4.0, 4.0)
    return table_base


def block_levels(rng, shape, cuts, low, largest):
    level, own = 1.0, jax.random.fold_in(rng, 6)
    for axis_at, blocks in cuts:
        steps = jnp.exp(jax.random.uniform(jax.random.fold_in(own, axis_at), (blocks,), jnp.float32, low / len(cuts), largest / len(cuts)))
        level = level * jnp.repeat(steps, shape[axis_at] // blocks).reshape([-1 if axis == axis_at else 1 for axis in range(len(shape))])
    return level


def scatter_about(own_key, extent, width, most, shards=(), kind=jnp.bfloat16):
    values = width * jax.random.normal(own_key, extent, jnp.float32)
    if shards:
        values = values * block_levels(own_key, extent, shards, -0.22, 0.18)
    return jnp.clip(values, -most, most).astype(kind)


def setup_inputs(seed: int = 0) -> dict:
    streams_of = jax.random.split(jax.random.key(seed), 13)
    return {
        "inputs": draw_inputs(jax.random.fold_in(streams_of[12], 71), 0),
        "cotangent": scatter_about(streams_of[1], (NLAT, NLON, CH), 1.0, 6.0, ((0, 16), (1, 16))),
        "valid_cells": draw_valid_cells(jax.random.fold_in(streams_of[12], 71), 0),
        "gain_one": jnp.clip(1.0 + 0.18 * jax.random.normal(streams_of[3], (CH,), jnp.float32), 0.1, 1.9),
        "shift_one": scatter_about(streams_of[4], (CH,), 0.5, 2.0, (), jnp.float32),
        "gain_two": jnp.clip(1.0 + 0.18 * jax.random.normal(streams_of[5], (CH,), jnp.float32), 0.1, 1.9),
        "shift_two": scatter_about(streams_of[6], (CH,), 0.5, 2.0, (), jnp.float32),
        "qkv_weight": scatter_about(streams_of[7], (CH, 3 * CH), CH ** -0.5, 0.375),
        "proj_weight": scatter_about(streams_of[8], (CH, CH), CH ** -0.5, 0.375),
        "up_weight": scatter_about(streams_of[9], (CH, MLP), CH ** -0.5, 0.375),
        "down_weight": scatter_about(streams_of[10], (MLP, CH), MLP ** -0.5, 0.1875),
        "bias_table": draw_bias_table(jax.random.fold_in(streams_of[12], 71), 0),
    }


EPSILON = 1e-05
ROOT_HALF = 0.7071067811865476
INV_ROOT_TAU = 0.3989422804014327

def widen(values):
    return lax.optimization_barrier(values).astype(jnp.float32)

def norm_rows(values, gain_vec, shift_vec):
    row_mean = lax.optimization_barrier(jnp.mean(values, axis=-1, keepdims=True))
    centred = values - row_mean
    inv_std = lax.rsqrt(lax.optimization_barrier(jnp.mean(centred * centred, axis=-1, keepdims=True)) + EPSILON)
    normed = centred * inv_std
    return (normed * gain_vec + shift_vec, normed, inv_std)

def norm_back(upstream, normed, inv_std, gain_vec):
    scaled = upstream * gain_vec
    return inv_std * (scaled - lax.optimization_barrier(jnp.mean(scaled, axis=-1, keepdims=True)) - normed * lax.optimization_barrier(jnp.mean(scaled * normed, axis=-1, keepdims=True)))

def gelu_exact(values):
    return 0.5 * values * (1.0 + lax.erf(values * ROOT_HALF))

def gelu_slope(values):
    return 0.5 * (1.0 + lax.erf(values * ROOT_HALF)) + values * jnp.exp(-0.5 * values * values) * INV_ROOT_TAU

def to_windows(field):
    row_count, col_count, feats = field.shape
    blocks = field.reshape(row_count // WIN, WIN, col_count // WIN, WIN, feats).transpose(0, 2, 1, 3, 4)
    return blocks.reshape(row_count // WIN, col_count // WIN, WIN * WIN, feats)

def from_windows(blocks):
    win_rows, win_cols, cells_in, feats = blocks.shape
    field = blocks.reshape(win_rows, win_cols, WIN, WIN, feats).transpose(0, 2, 1, 3, 4)
    return field.reshape(win_rows * WIN, win_cols * WIN, feats)

def relative_index():
    cell_ids = jnp.arange(WIN * WIN, dtype=jnp.int32)
    row_pos = cell_ids // WIN
    col_pos = cell_ids % WIN
    index_grid = (row_pos[:, None] - row_pos[None, :] + WIN - 1) * (2 * WIN - 1) + col_pos[:, None] - col_pos[None, :] + WIN - 1
    return index_grid.reshape(-1).astype(jnp.int32)

def attend(qkv_win, keys_ok, bias_full):
    win_total, win_cells, triple = qkv_win.shape
    pieces = qkv_win.reshape(win_total, win_cells, 3, HEADS, HEAD_DIM)
    queries = widen(pieces[:, :, 0])
    keys_in = widen(pieces[:, :, 1])
    values_in = widen(pieces[:, :, 2])
    scores = jnp.einsum('nihd,njhd->nhij', queries, keys_in) * HEAD_DIM ** (-0.5) + bias_full
    allowed = keys_ok[:, None, None, :] | jnp.eye(win_cells, dtype=bool)
    scores = jnp.where(allowed, scores, -jnp.inf)
    weights = jnp.exp(scores - lax.optimization_barrier(jnp.max(scores, axis=-1, keepdims=True)))
    attn_probs = weights / lax.optimization_barrier(jnp.sum(weights, axis=-1, keepdims=True))
    mixed = jnp.einsum('nhij,njhd->nihd', widen(attn_probs.astype(jnp.bfloat16)), values_in)
    return (mixed.reshape(win_total, win_cells, HEADS * HEAD_DIM).astype(jnp.bfloat16), attn_probs)

def attend_back(qkv_win, attn_probs, grad_mixed):
    win_total, win_cells, triple = qkv_win.shape
    pieces = qkv_win.reshape(win_total, win_cells, 3, HEADS, HEAD_DIM)
    queries = widen(pieces[:, :, 0])
    keys_in = widen(pieces[:, :, 1])
    values_in = widen(pieces[:, :, 2])
    upstream = widen(grad_mixed.reshape(win_total, win_cells, HEADS, HEAD_DIM))
    grad_probs = jnp.einsum('nihd,njhd->nhij', upstream, values_in)
    grad_values = jnp.einsum('nhij,nihd->njhd', widen(attn_probs.astype(jnp.bfloat16)), upstream)
    grad_scores = attn_probs * (grad_probs - lax.optimization_barrier(jnp.sum(attn_probs * grad_probs, axis=-1, keepdims=True)))
    scores_low = widen(grad_scores.astype(jnp.bfloat16))
    factor = HEAD_DIM ** (-0.5)
    grad_queries = jnp.einsum('nhij,njhd->nihd', scores_low, keys_in) * factor
    grad_keys = jnp.einsum('nhij,nihd->njhd', scores_low, queries) * factor
    stacked = jnp.stack([grad_queries, grad_keys, grad_values], axis=2)
    return (stacked.reshape(win_total, win_cells, triple).astype(jnp.bfloat16), grad_scores)

def reference(inputs, cotangent, valid_cells, gain_one, shift_one, gain_two, shift_two, qkv_weight, proj_weight, up_weight, down_weight, bias_table):
    rim_width = WIN // 2
    grad_scale = 1.0 / math.sqrt(TOKENS)
    band_count = NLAT // WIN + 1
    tokens_wide = inputs.reshape(-1, CH).astype(jnp.float32)
    normed_one, hat_one, inv_one = norm_rows(tokens_wide, gain_one, shift_one)
    first_in = normed_one.astype(jnp.bfloat16)

    def shifted(field):
        rolled = jnp.roll(field, rim_width, axis=1)
        padded = jnp.pad(rolled, ((rim_width, rim_width), (0, 0), (0, 0)))
        return padded.reshape(band_count, WIN, NLON, field.shape[-1])

    def unshifted(field):
        whole = field.reshape(NLAT + 2 * rim_width, NLON, -1)[rim_width:rim_width + NLAT]
        return jnp.roll(whole, -rim_width, axis=1).reshape(TOKENS, -1)
    first_bands = shifted(first_in.reshape(NLAT, NLON, CH))
    ok_bands = shifted(valid_cells.reshape(NLAT, NLON, 1))[..., 0] > 0
    bias_full = bias_table[:, relative_index()].reshape(HEADS, WIN * WIN, WIN * WIN)

    def band_attend(band, band_ok):
        qkv_rows = jnp.dot(band.reshape(-1, CH), qkv_weight, preferred_element_type=jnp.float32).astype(jnp.bfloat16)
        qkv_win = to_windows(qkv_rows.reshape(WIN, NLON, 3 * CH))[0]
        keys_ok = to_windows(band_ok[..., None])[0, ..., 0]
        mixed, attn_probs = attend(qkv_win, keys_ok, bias_full)
        return (qkv_win, attn_probs, mixed)

    def forward_band(packed):
        qkv_win, attn_probs, mixed = band_attend(packed[0], packed[1])
        return from_windows(mixed[None])
    mixed_field = unshifted(lax.map(forward_band, (first_bands, ok_bands)))
    resid = (tokens_wide + jnp.dot(mixed_field, proj_weight, preferred_element_type=jnp.float32)).astype(jnp.bfloat16)

    def mlp_band(carry, packed):
        resid_band, grad_band = packed
        normed_two, hat_two, inv_two = norm_rows(resid_band.astype(jnp.float32), gain_two, shift_two)
        second_in = normed_two.astype(jnp.bfloat16)
        raised = jnp.dot(second_in, up_weight, preferred_element_type=jnp.float32)
        hidden = gelu_exact(raised).astype(jnp.bfloat16)
        out_band = (resid_band.astype(jnp.float32) + jnp.dot(hidden, down_weight, preferred_element_type=jnp.float32)).astype(jnp.bfloat16)
        d_raised = (jnp.dot(grad_band, down_weight.T, preferred_element_type=jnp.float32) * gelu_slope(raised)).astype(jnp.bfloat16)
        d_second = jnp.dot(d_raised, up_weight.T, preferred_element_type=jnp.float32)
        d_resid = (grad_band.astype(jnp.float32) + norm_back(d_second, hat_two, inv_two, gain_two)).astype(jnp.bfloat16)
        totals = (carry[0] + jnp.dot(second_in.T, d_raised, preferred_element_type=jnp.float32), carry[1] + jnp.dot(hidden.T, grad_band, preferred_element_type=jnp.float32), carry[2] + lax.optimization_barrier(jnp.sum(d_second * hat_two, axis=0)), carry[3] + lax.optimization_barrier(jnp.sum(d_second, axis=0)))
        return (totals, (out_band, d_resid))
    start_mlp = (jnp.zeros((CH, MLP), jnp.float32), jnp.zeros((MLP, CH), jnp.float32), jnp.zeros((CH,), jnp.float32), jnp.zeros((CH,), jnp.float32))
    mlp_totals, (output, d_resid) = lax.scan(mlp_band, start_mlp, (resid.reshape(NLAT // WIN, -1, CH), cotangent.reshape(NLAT // WIN, -1, CH)))
    output = output.reshape(NLAT, NLON, CH)
    d_resid = d_resid.reshape(-1, CH)
    grad_proj = jnp.dot(mixed_field.T, d_resid, preferred_element_type=jnp.float32) * grad_scale
    d_mixed = jnp.dot(d_resid, proj_weight.T, preferred_element_type=jnp.float32).astype(jnp.bfloat16)
    grad_bands = shifted(d_mixed.reshape(NLAT, NLON, CH))

    def back_band(carry, packed):
        band, band_ok, grad_band = packed
        qkv_win, attn_probs, mixed = band_attend(band, band_ok)
        grad_win, grad_scores = attend_back(qkv_win, attn_probs, to_windows(grad_band)[0])
        d_qkv = from_windows(grad_win[None]).reshape(-1, 3 * CH)
        qkv_total = carry[0] + jnp.dot(band.reshape(-1, CH).T, d_qkv, preferred_element_type=jnp.float32)
        d_first = jnp.dot(d_qkv, qkv_weight.T, preferred_element_type=jnp.float32)
        return ((qkv_total, carry[1] + lax.optimization_barrier(jnp.sum(grad_scores, axis=0))), d_first.reshape(WIN, NLON, CH))
    start_attn = (jnp.zeros((CH, 3 * CH), jnp.float32), jnp.zeros((HEADS, WIN * WIN, WIN * WIN), jnp.float32))
    (qkv_total, score_total), first_bands_grad = lax.scan(back_band, start_attn, (first_bands, ok_bands, grad_bands))
    d_first = unshifted(first_bands_grad)
    grad_table = jnp.zeros((HEADS, (2 * WIN - 1) * (2 * WIN - 1)), jnp.float32).at[:, relative_index()].add(score_total.reshape(HEADS, -1)) * grad_scale
    grad_inputs = (d_resid.astype(jnp.float32) + norm_back(d_first, hat_one, inv_one, gain_one)).astype(jnp.bfloat16)
    return (output, grad_inputs.reshape(NLAT, NLON, CH), qkv_total * grad_scale, grad_proj, mlp_totals[0] * grad_scale, mlp_totals[1] * grad_scale, lax.optimization_barrier(jnp.sum(d_first * hat_one, axis=0)) * grad_scale, lax.optimization_barrier(jnp.sum(d_first, axis=0)) * grad_scale, mlp_totals[2] * grad_scale, mlp_totals[3] * grad_scale, grad_table)
```

```python
import math

import jax
import jax.numpy as jnp
from jax import lax
from jax.sharding import PartitionSpec as P

WIN = 8


EPSILON = 1e-05
ROOT_HALF = 0.7071067811865476
INV_ROOT_TAU = 0.3989422804014327


def norm_rows(values, gain_vec, shift_vec):
    row_mean = jnp.mean(values, axis=-1, keepdims=True)
    centred = values - row_mean
    inv_std = lax.rsqrt(jnp.mean(centred * centred, axis=-1, keepdims=True) + EPSILON)
    normed = centred * inv_std
    return (normed * gain_vec + shift_vec, normed, inv_std)


def norm_back(upstream, normed, inv_std, gain_vec):
    scaled = upstream * gain_vec
    return inv_std * (
        scaled
        - jnp.mean(scaled, axis=-1, keepdims=True)
        - normed * jnp.mean(scaled * normed, axis=-1, keepdims=True)
    )


def gelu_exact(values):
    return 0.5 * values * (1.0 + lax.erf(values * ROOT_HALF))


def gelu_slope(values):
    return (
        0.5 * (1.0 + lax.erf(values * ROOT_HALF))
        + values * jnp.exp(-0.5 * values * values) * INV_ROOT_TAU
    )


def to_windows(field):
    row_count, col_count, feats = field.shape
    blocks = field.reshape(row_count // WIN, WIN, col_count // WIN, WIN, feats).transpose(
        0, 2, 1, 3, 4
    )
    return blocks.reshape(row_count // WIN, col_count // WIN, WIN * WIN, feats)


def from_windows(blocks):
    win_rows, win_cols, cells_in, feats = blocks.shape
    field = blocks.reshape(win_rows, win_cols, WIN, WIN, feats).transpose(0, 2, 1, 3, 4)
    return field.reshape(win_rows * WIN, win_cols * WIN, feats)


def relative_index():
    cell_ids = jnp.arange(WIN * WIN, dtype=jnp.int32)
    row_pos = cell_ids // WIN
    col_pos = cell_ids % WIN
    index_grid = (
        (row_pos[:, None] - row_pos[None, :] + WIN - 1) * (2 * WIN - 1)
        + col_pos[:, None]
        - col_pos[None, :]
        + WIN
        - 1
    )
    return index_grid.reshape(-1)


def across(left, right):
    return lax.dot_general(
        left, right, (((0,), (0,)), ((), ())), preferred_element_type=jnp.float32
    )


def against(left, weight):
    return lax.dot_general(
        left, weight, (((1,), (1,)), ((), ())), preferred_element_type=jnp.float32
    )


def split_heads(qkv_win, head_count):
    win_total, win_cells, triple = qkv_win.shape
    pieces = qkv_win.reshape(win_total, win_cells, 3, head_count, triple // (3 * head_count))
    return (pieces[:, :, 0], pieces[:, :, 1], pieces[:, :, 2])


def attend(qkv_win, keys_ok, same_side, bias_full, head_count):
    win_total, win_cells, triple = qkv_win.shape
    queries, keys_in, values_in = split_heads(qkv_win, head_count)
    factor = queries.shape[-1] ** (-0.5)
    scores = (
        jnp.einsum("nihd,njhd->nhij", queries, keys_in, preferred_element_type=jnp.float32) * factor
        + bias_full
    )
    allowed = (keys_ok[:, None, None, :] | jnp.eye(win_cells, dtype=bool)) & same_side
    scores = jnp.where(allowed, scores, -jnp.inf)
    weights = jnp.exp(scores - jnp.max(scores, axis=-1, keepdims=True))
    attn_probs = weights / jnp.sum(weights, axis=-1, keepdims=True)
    mixed = jnp.einsum(
        "nhij,njhd->nihd",
        attn_probs.astype(jnp.bfloat16),
        values_in,
        preferred_element_type=jnp.float32,
    )
    return (mixed.reshape(win_total, win_cells, triple // 3).astype(jnp.bfloat16), attn_probs)


def attend_back(qkv_win, attn_probs, grad_mixed, head_count):
    win_total, win_cells, triple = qkv_win.shape
    queries, keys_in, values_in = split_heads(qkv_win, head_count)
    factor = queries.shape[-1] ** (-0.5)
    upstream = grad_mixed.reshape(queries.shape)
    grad_probs = jnp.einsum(
        "nihd,njhd->nhij", upstream, values_in, preferred_element_type=jnp.float32
    )
    grad_values = jnp.einsum(
        "nhij,nihd->njhd",
        attn_probs.astype(jnp.bfloat16),
        upstream,
        preferred_element_type=jnp.float32,
    )
    grad_scores = attn_probs * (
        grad_probs - jnp.sum(attn_probs * grad_probs, axis=-1, keepdims=True)
    )
    scores_low = grad_scores.astype(jnp.bfloat16)
    grad_queries = (
        jnp.einsum("nhij,njhd->nihd", scores_low, keys_in, preferred_element_type=jnp.float32)
        * factor
    )
    grad_keys = (
        jnp.einsum("nhij,nihd->njhd", scores_low, queries, preferred_element_type=jnp.float32)
        * factor
    )
    stacked = jnp.stack([grad_queries, grad_keys, grad_values], axis=2)
    return (stacked.reshape(win_total, win_cells, triple).astype(jnp.bfloat16), grad_scores)


LAT = ("xl", "y", "c")
LON = ("xh", "z")
EVERY = LAT + LON
CHIPS = ("xl", "y", "xh", "z")
SIDE = 16
CHUNK_ROWS = 16


def moved(block, lat_step, lon_step):
    pairs = []
    for lat in range(SIDE):
        for lon in range(SIDE):
            target = ((lat + lat_step) % SIDE) * SIDE + (lon + lon_step) % SIDE
            pairs.append((lat * SIDE + lon, target))
    return lax.ppermute(block, EVERY, pairs)


def shift_in(block):
    rows, cols, _ = block.shape
    half = WIN // 2
    above = moved(block[rows - half :, : cols - half], 1, 0)
    beside = moved(block[: rows - half, cols - half :], 0, 1)
    corner = moved(block[rows - half :, cols - half :], 1, 1)
    top = jnp.concatenate([corner, above], axis=1)
    low = jnp.concatenate([beside, block[: rows - half, : cols - half]], axis=1)
    return jnp.concatenate([top, low], axis=0)


def shift_out(block):
    half = WIN // 2
    below = moved(block[:half, half:], -1, 0)
    beside = moved(block[half:, :half], 0, -1)
    corner = moved(block[:half, :half], -1, -1)
    top = jnp.concatenate([block[half:, half:], beside], axis=1)
    low = jnp.concatenate([below, corner], axis=1)
    return jnp.concatenate([top, low], axis=0)


def local_cells(valid_cells, rows, cols, lat, lon):
    half = WIN // 2
    total_rows, total_cols = valid_cells.shape
    row_low = lax.rem(lat * rows + total_rows - half, total_rows)
    col_low = lax.rem(lon * cols + total_cols - half, total_cols)
    top = lax.dynamic_slice(valid_cells, (row_low, 0), (half, total_cols))
    low = lax.dynamic_slice(valid_cells, (lat * rows, 0), (rows - half, total_cols))
    band = jnp.concatenate([top, low], axis=0)
    left = lax.dynamic_slice(band, (0, col_low), (rows, half))
    right = lax.dynamic_slice(band, (0, lon * cols), (rows, cols - half))
    return jnp.concatenate([left, right], axis=1)


def reduce_all(grads):
    rows, lanes = grads.shape
    chips = lax.axis_size(CHIPS)
    halves = grads.reshape(2, rows // 2, lanes)
    first = lax.axis_index("c") == 0
    swap = [(0, 1), (1, 0)]
    keep = jnp.where(first, halves[0], halves[1])
    give = jnp.where(first, halves[1], halves[0]).astype(jnp.bfloat16)
    pair = (keep + lax.ppermute(give, "c", swap).astype(jnp.float32)).astype(jnp.bfloat16)
    pieces = lax.all_to_all(
        pair.reshape(chips, rows // (2 * chips), lanes), CHIPS, 0, 0, tiled=True
    )
    total = jnp.sum(pieces.astype(jnp.float32), axis=0).astype(jnp.bfloat16)
    spread = lax.all_to_all(
        jnp.broadcast_to(total[None], (chips,) + total.shape), CHIPS, 0, 0, tiled=True
    ).reshape(rows // 2, lanes)
    other = lax.ppermute(spread, "c", swap)
    return jnp.concatenate(
        [jnp.where(first, spread, other), jnp.where(first, other, spread)], axis=0
    )


def per_device(
    inputs,
    cotangent,
    valid_cells,
    gain_one,
    shift_one,
    gain_two,
    shift_two,
    qkv_weight,
    proj_weight,
    up_weight,
    down_weight,
    bias_table,
):
    row_count, col_count, channels = inputs.shape
    head_count = bias_table.shape[0]
    win_cells = WIN * WIN
    lat_place = lax.axis_index(LAT)
    lon_place = lax.axis_index(LON)
    grad_scale = 1.0 / math.sqrt(row_count * col_count * lax.axis_size(EVERY))
    both = shift_in(jnp.concatenate([inputs, cotangent], axis=-1))
    windows = to_windows(both).reshape(-1, 2 * channels)
    upstream = windows[:, channels:]
    cells = local_cells(valid_cells, row_count, col_count, lat_place, lon_place)
    keys_ok = to_windows(cells[..., None])[..., 0].reshape(-1, win_cells) > 0
    tokens_wide = windows[:, :channels].astype(jnp.float32)
    normed_one, hat_one, inv_one = norm_rows(tokens_wide, gain_one, shift_one)
    first_in = normed_one.astype(jnp.bfloat16)
    qkv_win = jnp.dot(first_in, qkv_weight, preferred_element_type=jnp.float32).astype(jnp.bfloat16)
    qkv_win = qkv_win.reshape(-1, win_cells, 3 * channels)
    entries = bias_table.shape[1]
    chooser = (relative_index()[:, None] == jnp.arange(entries, dtype=jnp.int32)[None, :]).astype(
        jnp.float32
    )
    bias_full = jnp.dot(bias_table, chooser.T, precision=lax.Precision.HIGHEST).reshape(
        head_count, win_cells, win_cells
    )
    upper = jnp.arange(win_cells) < win_cells // 2
    same_side = (upper[:, None] == upper[None, :]) | (lat_place > 0)
    mixed_win, attn_probs = attend(qkv_win, keys_ok, same_side, bias_full, head_count)
    mixed = mixed_win.reshape(-1, channels)
    resid = (tokens_wide + jnp.dot(mixed, proj_weight, preferred_element_type=jnp.float32)).astype(
        jnp.bfloat16
    )
    normed_two, hat_two, inv_two = norm_rows(resid.astype(jnp.float32), gain_two, shift_two)
    second_in = normed_two.astype(jnp.bfloat16)
    raised = jnp.dot(second_in, up_weight, preferred_element_type=jnp.float32)
    hidden = gelu_exact(raised).astype(jnp.bfloat16)
    output = (
        resid.astype(jnp.float32) + jnp.dot(hidden, down_weight, preferred_element_type=jnp.float32)
    ).astype(jnp.bfloat16)
    d_raised = (against(upstream, down_weight) * gelu_slope(raised)).astype(jnp.bfloat16)
    grad_down = across(hidden, upstream) * grad_scale
    grad_up = across(second_in, d_raised) * grad_scale
    d_second = against(d_raised, up_weight)
    grad_gain_two = jnp.sum(d_second * hat_two, axis=0) * grad_scale
    grad_shift_two = jnp.sum(d_second, axis=0) * grad_scale
    d_resid = (
        upstream.astype(jnp.float32) + norm_back(d_second, hat_two, inv_two, gain_two)
    ).astype(jnp.bfloat16)
    grad_proj = across(mixed, d_resid) * grad_scale
    d_mixed = against(d_resid, proj_weight).astype(jnp.bfloat16)
    grad_win, grad_scores = attend_back(
        qkv_win, attn_probs, d_mixed.reshape(-1, win_cells, channels), head_count
    )
    score_total = jnp.sum(grad_scores, axis=0)
    grad_table = (
        jnp.dot(score_total.reshape(head_count, -1), chooser, precision=lax.Precision.HIGHEST)
        * grad_scale
    )
    d_qkv = grad_win.reshape(-1, 3 * channels)
    grad_qkv = across(first_in, d_qkv) * grad_scale
    d_first = against(d_qkv, qkv_weight)
    grad_gain_one = jnp.sum(d_first * hat_one, axis=0) * grad_scale
    grad_shift_one = jnp.sum(d_first, axis=0) * grad_scale
    grad_inputs = (
        d_resid.astype(jnp.float32) + norm_back(d_first, hat_one, inv_one, gain_one)
    ).astype(jnp.bfloat16)
    def shape_back(rows_win):
        field = from_windows(rows_win.reshape(1, -1, win_cells, rows_win.shape[-1]))
        return shift_out(field)

    table_rows = jnp.pad(grad_table, ((0, 0), (0, channels - entries)))
    vectors = jnp.stack([grad_gain_one, grad_shift_one, grad_gain_two, grad_shift_two])
    parts = [grad_down]
    parts += [grad_up[:, at : at + channels] for at in range(0, grad_up.shape[1], channels)]
    parts += [grad_qkv[:, at : at + channels] for at in range(0, grad_qkv.shape[1], channels)]
    parts += [grad_proj, vectors, table_rows]
    packed = jnp.concatenate(parts, axis=0)
    block = lax.axis_size(EVERY) * CHUNK_ROWS
    packed = jnp.pad(packed, ((0, -packed.shape[0] % block), (0, 0)))
    wide = shape_back(jnp.concatenate([output, grad_inputs], axis=-1))
    sums = reduce_all(packed).astype(jnp.float32)
    places = [0]
    for part in parts:
        places.append(places[-1] + part.shape[0])
    found = [sums[low:high] for low, high in zip(places, places[1:])]
    up_parts = grad_up.shape[1] // channels
    qkv_parts = grad_qkv.shape[1] // channels
    up_sum = jnp.concatenate(found[1 : 1 + up_parts], axis=1)
    qkv_sum = jnp.concatenate(found[1 + up_parts : 1 + up_parts + qkv_parts], axis=1)
    return (
        wide[..., :channels],
        wide[..., channels:],
        qkv_sum,
        found[-3],
        up_sum,
        found[0],
        found[-2][0],
        found[-2][1],
        found[-2][2],
        found[-2][3],
        found[-1][:, :entries],
    )


def solution(mesh):
    split = jax.sharding.Mesh(mesh.devices.reshape(2, 4, 2, 2, 8), EVERY)
    placed = (
        P(LAT, LON, None),
        P(LAT, LON, None),
        P(),
        P(),
        P(),
        P(),
        P(),
        P(),
        P(),
        P(),
        P(),
        P(),
    )
    return jax.shard_map(
        per_device,
        mesh=split,
        in_specs=placed,
        out_specs=(
            P(LAT, LON, None),
            P(LAT, LON, None),
            P(),
            P(),
            P(),
            P(),
            P(),
            P(),
            P(),
            P(),
            P(),
        ),
        check_vma=False,
    )
```

```python
import functools
import math

import jax
import jax.numpy as jnp
from jax import lax
from jax.experimental import pallas as pl
from jax.experimental.pallas import tpu as pltpu
from jax.sharding import PartitionSpec as P

WIN = 8
CELLS = WIN * WIN
HALF = WIN // 2
CH = 256
HEADS = 8
HEAD_DIM = 32
MLP = 1024
ROWS = 8
COLS = 64
WINDOWS = COLS // WIN
LOCAL = ROWS * COLS
PAIRS = HEADS * CELLS
ENTRIES = (2 * WIN - 1) * (2 * WIN - 1)

EPSILON = 1e-05
ROOT_HALF = 0.7071067811865476
INV_ROOT_TAU = 0.3989422804014327
NEVER = -1e30

LAT = ("xl", "y", "c")
LON = ("xh", "z")
EVERY = LAT + LON
PLANE = ("xl", "y", "xh")
SIDE = 16

AT_UP = MLP
AT_QKV = 2 * MLP
AT_PROJ = 2 * MLP + 3 * CH
AT_SMALL = 3 * MLP
SMALL = 16
PIECE = 104
PLANE_SIZE = 16
CORE_ROWS = PIECE * PLANE_SIZE
PACK_ROWS = 2 * CORE_ROWS

f32 = jnp.float32
bf16 = jnp.bfloat16


def moved(block, lat_step, lon_step):
    pairs = []
    for lat in range(SIDE):
        for lon in range(SIDE):
            target = ((lat + lat_step) % SIDE) * SIDE + (lon + lon_step) % SIDE
            pairs.append((lat * SIDE + lon, target))
    return lax.ppermute(block, EVERY, pairs)


def local_cells(valid_cells, lat, lon):
    total_rows, total_cols = valid_cells.shape
    row_low = lax.rem(lat * ROWS + total_rows - HALF, total_rows)
    col_low = lax.rem(lon * COLS + total_cols - HALF, total_cols)
    top = lax.dynamic_slice(valid_cells, (row_low, 0), (HALF, total_cols))
    low = lax.dynamic_slice(valid_cells, (lat * ROWS, 0), (ROWS - HALF, total_cols))
    band = jnp.concatenate([top, low], axis=0)
    left = lax.dynamic_slice(band, (0, col_low), (ROWS, HALF))
    right = lax.dynamic_slice(band, (0, lon * COLS), (ROWS, COLS - HALF))
    return jnp.concatenate([left, right], axis=1)


def relative_index():
    cell_ids = jnp.arange(CELLS, dtype=jnp.int32)
    row_pos = cell_ids // WIN
    col_pos = cell_ids % WIN
    return (
        (row_pos[:, None] - row_pos[None, :] + WIN - 1) * (2 * WIN - 1)
        + col_pos[:, None]
        - col_pos[None, :]
        + WIN
        - 1
    )


def dot(left, right):
    return jnp.dot(left, right, preferred_element_type=f32)


def across(left, right):
    return lax.dot_general(left, right, (((0,), (0,)), ((), ())), preferred_element_type=f32)


def against(left, right):
    return lax.dot_general(left, right, (((1,), (1,)), ((), ())), preferred_element_type=f32)


def split_dot(left, right):
    high = left.astype(bf16)
    low = (left - high.astype(f32)).astype(bf16)
    return dot(high, right) + dot(low, right)


def row_stats(values):
    centred = values - jnp.mean(values, axis=-1, keepdims=True)
    inv_std = lax.rsqrt(jnp.mean(centred * centred, axis=-1, keepdims=True) + EPSILON)
    return centred * inv_std, inv_std


def norm_back(upstream, normed, inv_std, gain_vec):
    scaled = upstream * gain_vec
    return inv_std * (
        scaled
        - jnp.mean(scaled, axis=-1, keepdims=True)
        - normed * jnp.mean(scaled * normed, axis=-1, keepdims=True)
    )


def block_kernel(
    place_ref,
    inputs_ref,
    cotangent_ref,
    above_ref,
    beside_ref,
    corner_ref,
    valid_ref,
    gain_one_ref,
    shift_one_ref,
    gain_two_ref,
    shift_two_ref,
    qkv_weight_ref,
    proj_weight_ref,
    up_weight_ref,
    down_weight_ref,
    bias_ref,
    pick_one_ref,
    pick_two_ref,
    output_ref,
    grad_inputs_ref,
    below_ref,
    side_ref,
    edge_ref,
    keep_ref,
    give_ref,
    wide,
    tokens,
    upstream,
    hat_one,
    first_in,
    qkv,
    probs,
    mixed,
    second_in,
    total_out,
    total_back,
    d_resid,
    d_mixed,
    d_qkv,
    head_rows,
    score_total,
    score_rows,
    table_mid,
    packed,
):
    scale = 1.0 / math.sqrt(LOCAL * SIDE * SIDE)
    factor = HEAD_DIM**-0.5
    lat = place_ref[0]
    core = place_ref[1]

    def assemble(own_ref, lanes, target):
        for a in range(ROWS):
            if a < HALF:
                wide[0:16, :] = corner_ref[a, :, lanes].astype(f32)
                wide[16 : 16 + COLS, :] = above_ref[a, :, lanes].astype(f32)
            else:
                wide[0:16, :] = beside_ref[a - HALF, :, lanes].astype(f32)
                wide[16 : 16 + COLS, :] = own_ref[a - HALF].astype(f32)
            line = wide[16 - HALF : 16 - HALF + COLS, :]
            for w in range(WINDOWS):
                target[w * CELLS + a * WIN : w * CELLS + (a + 1) * WIN, :] = line[
                    w * WIN : (w + 1) * WIN
                ].astype(target.dtype)

    assemble(inputs_ref, slice(0, CH), tokens)
    assemble(cotangent_ref, slice(CH, 2 * CH), total_back)
    upstream[...] = total_back[...].astype(bf16)

    lane_head = lax.broadcasted_iota(jnp.int32, (PAIRS, CH), 1) // HEAD_DIM
    row_head = lax.broadcasted_iota(jnp.int32, (PAIRS, CH), 0) // CELLS
    head_rows[...] = jnp.where(lane_head == row_head, 1.0, 0.0).astype(bf16)

    gain_one = gain_one_ref[...]
    normed, inv_one = row_stats(tokens[...])
    hat_one[...] = normed
    first = (normed * gain_one + shift_one_ref[...]).astype(bf16)
    first_in[...] = first
    qkv[...] = dot(first, qkv_weight_ref[...]).astype(bf16)

    def spread(block):
        return jnp.concatenate([block] * HEADS, axis=0) * head_rows[...]

    def gather(block):
        found = None
        lanes = lax.broadcasted_iota(jnp.int32, (1, CH), 1) // HEAD_DIM
        for h in range(HEADS):
            part = jnp.where(lanes == h, block[h * CELLS : (h + 1) * CELLS], 0.0)
            found = part if found is None else found + part
        return found

    key_id = lax.broadcasted_iota(jnp.int32, (CELLS, PAIRS), 0)
    query_id = lax.rem(lax.broadcasted_iota(jnp.int32, (CELLS, PAIRS), 1), CELLS)
    same_cell = key_id == query_id
    same_side = ((key_id < CELLS // 2) == (query_id < CELLS // 2)) | (lat > 0)

    def forward(w, carry):
        at = pl.multiple_of(w * CELLS, CELLS)
        rows = pl.ds(at, CELLS)
        queries = spread(qkv[rows, 0:CH])
        keys_in = qkv[rows, CH : 2 * CH]
        values_in = qkv[rows, 2 * CH : 3 * CH]
        scores = against(keys_in, queries) * factor + bias_ref[...]
        usable = jnp.concatenate([valid_ref[rows, :]] * (PAIRS // 128), axis=1) > 0.0
        scores = jnp.where((usable | same_cell) & same_side, scores, NEVER)
        weights = jnp.exp(scores - jnp.max(scores, axis=0, keepdims=True))
        share = weights * (1.0 / jnp.sum(weights, axis=0, keepdims=True))
        probs[rows, :] = share
        mixed[rows, :] = gather(across(share.astype(bf16), values_in)).astype(bf16)
        return carry

    lax.fori_loop(0, WINDOWS, forward, 0, unroll=2)

    resid = (tokens[...] + dot(mixed[...], proj_weight_ref[...])).astype(bf16).astype(f32)
    hat_two, inv_two = row_stats(resid)
    gain_two = gain_two_ref[...]
    second_in[...] = (hat_two * gain_two + shift_two_ref[...]).astype(bf16)
    total_out[...] = resid
    total_back[...] = jnp.zeros_like(total_back)

    def feed(k, carry):
        at = pl.multiple_of(k * CH, CH)
        cols = pl.ds(at, CH)
        up_part = up_weight_ref[:, cols]
        down_part = down_weight_ref[cols, :]
        second = second_in[...]
        grads = upstream[...]
        raised = dot(second, up_part)
        area = 0.5 * (1.0 + lax.erf(raised * ROOT_HALF))
        hidden = (raised * area).astype(bf16)
        slope = area + raised * jnp.exp(-0.5 * raised * raised) * INV_ROOT_TAU
        d_raised = (against(grads, down_part) * slope).astype(bf16)
        total_out[...] += dot(hidden, down_part)
        total_back[...] += against(d_raised, up_part)
        packed[cols, :] = (across(hidden, grads) * scale).astype(bf16)
        packed[pl.ds(AT_UP + at, CH), :] = (across(second, d_raised) * scale).astype(bf16)
        return carry

    lax.fori_loop(0, MLP // CH, feed, 0)

    def lay_out(values, out_ref, lanes):
        for a in range(ROWS):
            line = jnp.concatenate(
                [
                    values[w * CELLS + a * WIN : w * CELLS + (a + 1) * WIN]
                    for w in range(WINDOWS)
                ],
                axis=0,
            ).astype(bf16)
            out_ref[a] = line
            if a < HALF:
                below_ref[a, :, lanes] = line
                edge_ref[a, :, lanes] = line[:16]
            else:
                side_ref[a - HALF, :, lanes] = line[:16]

    lay_out(total_out[...], output_ref, slice(0, CH))

    d_second = total_back[...]
    grad_gain_two = jnp.sum(d_second * hat_two, axis=0, keepdims=True)
    grad_shift_two = jnp.sum(d_second, axis=0, keepdims=True)
    back = norm_back(d_second, hat_two, inv_two, gain_two)
    d_low = (upstream[...].astype(f32) + back).astype(bf16)
    d_resid[...] = d_low
    packed[AT_PROJ : AT_PROJ + CH, :] = (across(mixed[...], d_low) * scale).astype(bf16)
    d_mixed[...] = against(d_low, proj_weight_ref[...]).astype(bf16)
    score_total[...] = jnp.zeros_like(score_total)

    def backward(w, carry):
        at = pl.multiple_of(w * CELLS, CELLS)
        rows = pl.ds(at, CELLS)
        grads = spread(d_mixed[rows, :])
        queries = spread(qkv[rows, 0:CH])
        keys_in = qkv[rows, CH : 2 * CH]
        values_in = qkv[rows, 2 * CH : 3 * CH]
        share = probs[rows, :]
        d_share = against(values_in, grads)
        d_scores = share * (d_share - jnp.sum(share * d_share, axis=0, keepdims=True))
        score_total[...] += d_scores
        low = d_scores.astype(bf16)
        d_qkv[rows, 0:CH] = (gather(across(low, keys_in)) * factor).astype(bf16)
        d_qkv[rows, CH : 2 * CH] = (dot(low, queries) * factor).astype(bf16)
        d_qkv[rows, 2 * CH : 3 * CH] = dot(share.astype(bf16), grads).astype(bf16)
        return carry

    lax.fori_loop(0, WINDOWS, backward, 0, unroll=2)

    for part in range(3):
        lanes = slice(part * CH, (part + 1) * CH)
        found = across(first_in[...], d_qkv[:, lanes]) * scale
        packed[AT_QKV + part * CH : AT_QKV + (part + 1) * CH, :] = found.astype(bf16)
    d_first = against(d_qkv[...], qkv_weight_ref[...])
    normed = hat_one[...]
    grad_gain_one = jnp.sum(d_first * normed, axis=0, keepdims=True)
    grad_shift_one = jnp.sum(d_first, axis=0, keepdims=True)
    back = norm_back(d_first, normed, inv_one, gain_one)
    lay_out(d_resid[...].astype(f32) + back, grad_inputs_ref, slice(CH, 2 * CH))

    for h in range(HEADS):
        for a in range(WIN):
            score_rows[h * WIN : (h + 1) * WIN, a * CELLS : (a + 1) * CELLS] = score_total[
                a * WIN : (a + 1) * WIN, h * CELLS : (h + 1) * CELLS
            ]
    table_mid[...] = split_dot(score_rows[...], pick_one_ref[...])
    strips = [table_mid[pl.ds(b, HEADS, stride=WIN), :] for b in range(WIN)]
    table = split_dot(jnp.concatenate(strips, axis=1), pick_two_ref[...])
    small = jnp.concatenate(
        [table, grad_gain_one, grad_shift_one, grad_gain_two, grad_shift_two, jnp.zeros((4, CH), f32)],
        axis=0,
    )
    packed[AT_SMALL : AT_SMALL + SMALL, :] = (small * scale).astype(bf16)
    rest = PACK_ROWS - AT_SMALL - SMALL
    packed[AT_SMALL + SMALL : PACK_ROWS, :] = jnp.zeros((rest, CH), bf16)
    keep_ref[...] = packed[pl.ds(pl.multiple_of(core * CORE_ROWS, 16), CORE_ROWS), :]
    give_ref[...] = packed[pl.ds(pl.multiple_of((1 - core) * CORE_ROWS, 16), CORE_ROWS), :]


def finish_kernel(
    place_ref,
    mine_ref,
    other_ref,
    out_in_ref,
    grad_in_ref,
    below_ref,
    side_ref,
    edge_ref,
    output_ref,
    grad_inputs_ref,
    grad_qkv_ref,
    grad_proj_ref,
    grad_up_ref,
    grad_down_ref,
    gain_one_ref,
    shift_one_ref,
    gain_two_ref,
    shift_two_ref,
    table_ref,
    whole,
    wide,
):
    core = place_ref[1]
    whole[pl.ds(pl.multiple_of(core * CORE_ROWS, 16), CORE_ROWS), :] = mine_ref[...]
    whole[pl.ds(pl.multiple_of((1 - core) * CORE_ROWS, 16), CORE_ROWS), :] = other_ref[...]
    grad_down_ref[...] = whole[0:MLP, :].astype(f32)
    for k in range(MLP // CH):
        low = AT_UP + k * CH
        grad_up_ref[:, k * CH : (k + 1) * CH] = whole[low : low + CH, :].astype(f32)
    for k in range(3):
        low = AT_QKV + k * CH
        grad_qkv_ref[:, k * CH : (k + 1) * CH] = whole[low : low + CH, :].astype(f32)
    grad_proj_ref[...] = whole[AT_PROJ : AT_PROJ + CH, :].astype(f32)
    small = whole[AT_SMALL : AT_SMALL + SMALL, :].astype(f32)
    table_ref[...] = small[0:HEADS, 0:ENTRIES]
    gain_one_ref[...] = small[HEADS : HEADS + 1]
    shift_one_ref[...] = small[HEADS + 1 : HEADS + 2]
    gain_two_ref[...] = small[HEADS + 2 : HEADS + 3]
    shift_two_ref[...] = small[HEADS + 3 : HEADS + 4]
    for own_ref, out_ref, lanes in (
        (out_in_ref, output_ref, slice(0, CH)),
        (grad_in_ref, grad_inputs_ref, slice(CH, 2 * CH)),
    ):
        for a in range(ROWS):
            if a < HALF:
                wide[0:COLS, :] = own_ref[a + HALF].astype(f32)
                wide[COLS : COLS + 16, :] = side_ref[a, :, lanes].astype(f32)
            else:
                wide[0:COLS, :] = below_ref[a - HALF, :, lanes].astype(f32)
                wide[COLS : COLS + 16, :] = edge_ref[a - HALF, :, lanes].astype(f32)
            out_ref[a] = wide[HALF : HALF + COLS, :].astype(bf16)


def in_vmem():
    return pl.BlockSpec(memory_space=pltpu.VMEM)


def in_smem():
    return pl.BlockSpec(memory_space=pltpu.SMEM)


def shape(dims, dtype):
    return jax.ShapeDtypeStruct(dims, dtype)


def run_block(*operands):
    return pl.pallas_call(
        block_kernel,
        out_shape=(
            shape((ROWS, COLS, CH), bf16),
            shape((ROWS, COLS, CH), bf16),
            shape((HALF, COLS, 2 * CH), bf16),
            shape((HALF, 16, 2 * CH), bf16),
            shape((HALF, 16, 2 * CH), bf16),
            shape((CORE_ROWS, CH), bf16),
            shape((CORE_ROWS, CH), bf16),
        ),
        in_specs=[in_smem()] + [in_vmem()] * (len(operands) - 1),
        out_specs=[in_vmem()] * 7,
        scratch_shapes=[
            pltpu.VMEM((COLS + 16, CH), f32),
            pltpu.VMEM((LOCAL, CH), f32),
            pltpu.VMEM((LOCAL, CH), bf16),
            pltpu.VMEM((LOCAL, CH), f32),
            pltpu.VMEM((LOCAL, CH), bf16),
            pltpu.VMEM((LOCAL, 3 * CH), bf16),
            pltpu.VMEM((LOCAL, PAIRS), f32),
            pltpu.VMEM((LOCAL, CH), bf16),
            pltpu.VMEM((LOCAL, CH), bf16),
            pltpu.VMEM((LOCAL, CH), f32),
            pltpu.VMEM((LOCAL, CH), f32),
            pltpu.VMEM((LOCAL, CH), bf16),
            pltpu.VMEM((LOCAL, CH), bf16),
            pltpu.VMEM((LOCAL, 3 * CH), bf16),
            pltpu.VMEM((PAIRS, CH), bf16),
            pltpu.VMEM((CELLS, PAIRS), f32),
            pltpu.VMEM((CELLS, PAIRS), f32),
            pltpu.VMEM((CELLS, 128), f32),
            pltpu.VMEM((PACK_ROWS, CH), bf16),
        ],
        compiler_params=pltpu.CompilerParams(vmem_limit_bytes=48 * 1024 * 1024),
        cost_estimate=pl.CostEstimate(
            flops=4_000_000_000, bytes_accessed=8_000_000, transcendentals=2_000_000
        ),
    )(*operands)


def run_finish(*operands):
    return pl.pallas_call(
        finish_kernel,
        out_shape=(
            shape((ROWS, COLS, CH), bf16),
            shape((ROWS, COLS, CH), bf16),
            shape((CH, 3 * CH), f32),
            shape((CH, CH), f32),
            shape((CH, MLP), f32),
            shape((MLP, CH), f32),
            shape((1, CH), f32),
            shape((1, CH), f32),
            shape((1, CH), f32),
            shape((1, CH), f32),
            shape((HEADS, ENTRIES), f32),
        ),
        in_specs=[in_smem()] + [in_vmem()] * (len(operands) - 1),
        out_specs=[in_vmem()] * 11,
        scratch_shapes=[
            pltpu.VMEM((PACK_ROWS, CH), bf16),
            pltpu.VMEM((COLS + 16, CH), f32),
        ],
        compiler_params=pltpu.CompilerParams(vmem_limit_bytes=32 * 1024 * 1024),
        cost_estimate=pl.CostEstimate(flops=1_000_000, bytes_accessed=8_000_000, transcendentals=0),
    )(*operands)


def pickers():
    ids = jnp.arange(PAIRS, dtype=jnp.int32)
    low_a, high_a, b = ids // CELLS, (ids // WIN) % WIN, ids % WIN
    mid = jnp.arange(128, dtype=jnp.int32)
    pick_one = ((high_a - low_a + WIN - 1) * WIN + b)[:, None] == mid[None, :]
    deep = jnp.arange(1024, dtype=jnp.int32)
    low_b, step, high_b = deep // 128, (deep // WIN) % 16, deep % WIN
    place = step * (2 * WIN - 1) + high_b - low_b + WIN - 1
    entry = jnp.arange(CH, dtype=jnp.int32)
    pick_two = (place[:, None] == entry[None, :]) & (step < 2 * WIN - 1)[:, None]
    return pick_one.astype(bf16), pick_two.astype(bf16)


def full_bias(bias_table):
    wanted = relative_index().T.reshape(-1)
    chooser = (wanted[None, :] == jnp.arange(ENTRIES, dtype=jnp.int32)[:, None]).astype(f32)
    full = jnp.dot(bias_table, chooser, precision=lax.Precision.HIGHEST)
    return full.reshape(HEADS, CELLS, CELLS).transpose(1, 0, 2).reshape(CELLS, PAIRS)


def total_over_chips(keep, give):
    swap = [(0, 1), (1, 0)]
    pair = keep.astype(f32) + lax.ppermute(give, "c", swap).astype(f32)
    pieces = pair.astype(bf16).reshape(PLANE_SIZE, PIECE, CH)
    pieces = lax.all_to_all(pieces, PLANE, 0, 0, tiled=True)
    part = jnp.sum(pieces.astype(f32), axis=0).astype(bf16)
    depth = lax.axis_size("z")
    copies = jnp.broadcast_to(part[None], (depth, PIECE, CH))
    copies = lax.all_to_all(copies, "z", 0, 0, tiled=True)
    part = jnp.sum(copies.astype(f32), axis=0).astype(bf16)
    copies = jnp.broadcast_to(part[None], (PLANE_SIZE, PIECE, CH))
    mine = lax.all_to_all(copies, PLANE, 0, 0, tiled=True).reshape(CORE_ROWS, CH)
    return mine, lax.ppermute(mine, "c", swap)


def per_device(
    inputs,
    cotangent,
    valid_cells,
    gain_one,
    shift_one,
    gain_two,
    shift_two,
    qkv_weight,
    proj_weight,
    up_weight,
    down_weight,
    bias_table,
):
    lat = lax.axis_index(LAT)
    lon = lax.axis_index(LON)
    place = jnp.stack([lat, lax.axis_index("c")]).astype(jnp.int32)
    low_rows = jnp.concatenate([inputs[HALF:], cotangent[HALF:]], axis=-1)
    last = slice(COLS - 16, COLS)
    top_last = jnp.concatenate([inputs[:HALF, last], cotangent[:HALF, last]], axis=-1)
    above = moved(low_rows, 1, 0)
    beside = moved(top_last, 0, 1)
    corner = moved(low_rows[:, last], 1, 1)
    cells = local_cells(valid_cells, lat, lon)
    cells = cells.reshape(WIN, WINDOWS, WIN).transpose(1, 0, 2).reshape(LOCAL, 1)
    usable = jnp.broadcast_to((cells > 0).astype(f32), (LOCAL, 128))
    pick_one, pick_two = pickers()
    output, grad_inputs, below, side, edge, keep, give = run_block(
        place,
        inputs,
        cotangent,
        above,
        beside,
        corner,
        usable,
        gain_one.reshape(1, CH),
        shift_one.reshape(1, CH),
        gain_two.reshape(1, CH),
        shift_two.reshape(1, CH),
        qkv_weight,
        proj_weight,
        up_weight,
        down_weight,
        full_bias(bias_table),
        pick_one,
        pick_two,
    )
    below = moved(below, -1, 0)
    side = moved(side, 0, -1)
    edge = moved(edge, -1, -1)
    mine, other = total_over_chips(keep, give)
    found = run_finish(place, mine, other, output, grad_inputs, below, side, edge)
    return tuple(
        item.reshape(CH) if item.shape == (1, CH) else item for item in found
    )


def solution(mesh):
    split = jax.sharding.Mesh(mesh.devices.reshape(2, 4, 2, 2, 8), EVERY)
    field = P(LAT, LON, None)
    return jax.shard_map(
        per_device,
        mesh=split,
        in_specs=(field, field) + (P(),) * 10,
        out_specs=(field, field) + (P(),) * 9,
        check_vma=False,
    )
```

```python
import math

import jax
import jax.numpy as jnp
from jax import lax
from jax.experimental import pallas as pl
from jax.experimental.pallas import tpu as pltpu
from jax.sharding import PartitionSpec as P

WIN = 8
CELLS = WIN * WIN
HALF = WIN // 2
CH = 256
HEADS = 8
HEAD_DIM = 32
MLP = 1024
NLAT = 128
NLON = 1024
ROWS = 8
COLS = 64
WINDOWS = COLS // WIN
LOCAL = ROWS * COLS
PAIRS = HEADS * CELLS
ENTRIES = (2 * WIN - 1) * (2 * WIN - 1)

EPSILON = 1e-05
ROOT_HALF = 0.7071067811865476
INV_ROOT_TAU = 0.3989422804014327
NEVER = -1e30

LAT = ("xl", "y", "c")
LON = ("xh", "z")
EVERY = LAT + LON
PLANE = ("xl", "y", "xh")
SIDE = 16

AT_UP = MLP
AT_QKV = 2 * MLP
AT_PROJ = 2 * MLP + 3 * CH
AT_SMALL = 3 * MLP
SMALL = 16
PIECE = 104
PLANE_SIZE = 16
CORE_ROWS = PIECE * PLANE_SIZE
PACK_ROWS = 2 * CORE_ROWS

f32 = jnp.float32
bf16 = jnp.bfloat16


def moved(block, lat_step, lon_step):
    pairs = []
    for lat in range(SIDE):
        for lon in range(SIDE):
            target = ((lat + lat_step) % SIDE) * SIDE + (lon + lon_step) % SIDE
            pairs.append((lat * SIDE + lon, target))
    return lax.ppermute(block, EVERY, pairs)


def dot(left, right):
    return jnp.dot(left, right, preferred_element_type=f32)


def across(left, right):
    return lax.dot_general(left, right, (((0,), (0,)), ((), ())), preferred_element_type=f32)


def against(left, right):
    return lax.dot_general(left, right, (((1,), (1,)), ((), ())), preferred_element_type=f32)


def split_dot(left, right):
    high = left.astype(bf16)
    low = (left - high.astype(f32)).astype(bf16)
    return dot(high, right) + dot(low, right)


def row_stats(values):
    centred = values - jnp.mean(values, axis=-1, keepdims=True)
    inv_std = lax.rsqrt(jnp.mean(centred * centred, axis=-1, keepdims=True) + EPSILON)
    return centred * inv_std, inv_std


def norm_back(upstream, normed, inv_std, gain_vec):
    scaled = upstream * gain_vec
    return inv_std * (
        scaled
        - jnp.mean(scaled, axis=-1, keepdims=True)
        - normed * jnp.mean(scaled * normed, axis=-1, keepdims=True)
    )


def block_kernel(
    place_ref,
    inputs_ref,
    cotangent_ref,
    above_ref,
    beside_ref,
    corner_ref,
    valid_ref,
    gain_one_ref,
    shift_one_ref,
    gain_two_ref,
    shift_two_ref,
    qkv_weight_ref,
    proj_weight_ref,
    up_weight_ref,
    down_weight_ref,
    bias_ref,
    pick_one_ref,
    pick_two_ref,
    output_ref,
    grad_inputs_ref,
    below_ref,
    side_ref,
    edge_ref,
    keep_ref,
    give_ref,
    wide,
    tokens,
    upstream,
    hat_one,
    first_in,
    qkv,
    probs,
    mixed,
    second_in,
    total_out,
    total_back,
    d_resid,
    d_mixed,
    d_qkv,
    head_rows,
    score_total,
    score_rows,
    table_mid,
    packed,
):
    scale = 1.0 / math.sqrt(LOCAL * SIDE * SIDE)
    factor = HEAD_DIM**-0.5
    lat = place_ref[0]
    core = place_ref[1]

    def assemble(own_ref, lanes, target):
        for a in range(ROWS):
            if a < HALF:
                wide[0:16, :] = corner_ref[a, :, lanes].astype(f32)
                wide[16 : 16 + COLS, :] = above_ref[a, :, lanes].astype(f32)
            else:
                wide[0:16, :] = beside_ref[a - HALF, :, lanes].astype(f32)
                wide[16 : 16 + COLS, :] = own_ref[a - HALF].astype(f32)
            line = wide[16 - HALF : 16 - HALF + COLS, :]
            for w in range(WINDOWS):
                target[w * CELLS + a * WIN : w * CELLS + (a + 1) * WIN, :] = line[
                    w * WIN : (w + 1) * WIN
                ].astype(target.dtype)

    assemble(inputs_ref, slice(0, CH), tokens)
    assemble(cotangent_ref, slice(CH, 2 * CH), total_back)
    upstream[...] = total_back[...].astype(bf16)

    lane_head = lax.broadcasted_iota(jnp.int32, (PAIRS, CH), 1) // HEAD_DIM
    row_head = lax.broadcasted_iota(jnp.int32, (PAIRS, CH), 0) // CELLS
    head_rows[...] = jnp.where(lane_head == row_head, 1.0, 0.0).astype(bf16)

    gain_one = gain_one_ref[...]
    normed, inv_one = row_stats(tokens[...])
    hat_one[...] = normed
    first = (normed * gain_one + shift_one_ref[...]).astype(bf16)
    first_in[...] = first
    qkv[...] = dot(first, qkv_weight_ref[...]).astype(bf16)

    def spread(block):
        return jnp.concatenate([block] * HEADS, axis=0) * head_rows[...]

    def gather(block):
        found = None
        lanes = lax.broadcasted_iota(jnp.int32, (1, CH), 1) // HEAD_DIM
        for h in range(HEADS):
            part = jnp.where(lanes == h, block[h * CELLS : (h + 1) * CELLS], 0.0)
            found = part if found is None else found + part
        return found

    key_id = lax.broadcasted_iota(jnp.int32, (CELLS, PAIRS), 0)
    query_id = lax.rem(lax.broadcasted_iota(jnp.int32, (CELLS, PAIRS), 1), CELLS)
    same_cell = key_id == query_id
    same_side = ((key_id < CELLS // 2) == (query_id < CELLS // 2)) | (lat > 0)

    def forward(w, carry):
        at = pl.multiple_of(w * CELLS, CELLS)
        rows = pl.ds(at, CELLS)
        queries = spread(qkv[rows, 0:CH])
        keys_in = qkv[rows, CH : 2 * CH]
        values_in = qkv[rows, 2 * CH : 3 * CH]
        scores = against(keys_in, queries) * factor + bias_ref[...]
        usable = jnp.concatenate([valid_ref[rows, :]] * (PAIRS // 128), axis=1) > 0.0
        scores = jnp.where((usable | same_cell) & same_side, scores, NEVER)
        weights = jnp.exp(scores - jnp.max(scores, axis=0, keepdims=True))
        share = weights * (1.0 / jnp.sum(weights, axis=0, keepdims=True))
        probs[rows, :] = share
        mixed[rows, :] = gather(across(share.astype(bf16), values_in)).astype(bf16)
        return carry

    lax.fori_loop(0, WINDOWS, forward, 0, unroll=2)

    resid = (tokens[...] + dot(mixed[...], proj_weight_ref[...])).astype(bf16).astype(f32)
    hat_two, inv_two = row_stats(resid)
    gain_two = gain_two_ref[...]
    second_in[...] = (hat_two * gain_two + shift_two_ref[...]).astype(bf16)
    total_out[...] = resid
    total_back[...] = jnp.zeros_like(total_back)

    def feed(k, carry):
        at = pl.multiple_of(k * CH, CH)
        cols = pl.ds(at, CH)
        up_part = up_weight_ref[:, cols]
        down_part = down_weight_ref[cols, :]
        second = second_in[...]
        grads = upstream[...]
        raised = dot(second, up_part)
        area = 0.5 * (1.0 + lax.erf(raised * ROOT_HALF))
        hidden = (raised * area).astype(bf16)
        slope = area + raised * jnp.exp(-0.5 * raised * raised) * INV_ROOT_TAU
        d_raised = (against(grads, down_part) * slope).astype(bf16)
        total_out[...] += dot(hidden, down_part)
        total_back[...] += against(d_raised, up_part)
        packed[cols, :] = (across(hidden, grads) * scale).astype(bf16)
        packed[pl.ds(AT_UP + at, CH), :] = (across(second, d_raised) * scale).astype(bf16)
        return carry

    lax.fori_loop(0, MLP // CH, feed, 0)

    def lay_out(values, out_ref, lanes):
        for a in range(ROWS):
            line = jnp.concatenate(
                [
                    values[w * CELLS + a * WIN : w * CELLS + (a + 1) * WIN]
                    for w in range(WINDOWS)
                ],
                axis=0,
            ).astype(bf16)
            out_ref[a] = line
            if a < HALF:
                below_ref[a, :, lanes] = line
                edge_ref[a, :, lanes] = line[:16]
            else:
                side_ref[a - HALF, :, lanes] = line[:16]

    lay_out(total_out[...], output_ref, slice(0, CH))

    d_second = total_back[...]
    grad_gain_two = jnp.sum(d_second * hat_two, axis=0, keepdims=True)
    grad_shift_two = jnp.sum(d_second, axis=0, keepdims=True)
    back = norm_back(d_second, hat_two, inv_two, gain_two)
    d_low = (upstream[...].astype(f32) + back).astype(bf16)
    d_resid[...] = d_low
    packed[AT_PROJ : AT_PROJ + CH, :] = (across(mixed[...], d_low) * scale).astype(bf16)
    d_mixed[...] = against(d_low, proj_weight_ref[...]).astype(bf16)
    score_total[...] = jnp.zeros_like(score_total)

    def backward(w, carry):
        at = pl.multiple_of(w * CELLS, CELLS)
        rows = pl.ds(at, CELLS)
        grads = spread(d_mixed[rows, :])
        queries = spread(qkv[rows, 0:CH])
        keys_in = qkv[rows, CH : 2 * CH]
        values_in = qkv[rows, 2 * CH : 3 * CH]
        share = probs[rows, :]
        d_share = against(values_in, grads)
        d_scores = share * (d_share - jnp.sum(share * d_share, axis=0, keepdims=True))
        score_total[...] += d_scores
        low = d_scores.astype(bf16)
        d_qkv[rows, 0:CH] = (gather(across(low, keys_in)) * factor).astype(bf16)
        d_qkv[rows, CH : 2 * CH] = (dot(low, queries) * factor).astype(bf16)
        d_qkv[rows, 2 * CH : 3 * CH] = dot(share.astype(bf16), grads).astype(bf16)
        return carry

    lax.fori_loop(0, WINDOWS, backward, 0, unroll=2)

    for part in range(3):
        lanes = slice(part * CH, (part + 1) * CH)
        found = across(first_in[...], d_qkv[:, lanes]) * scale
        packed[AT_QKV + part * CH : AT_QKV + (part + 1) * CH, :] = found.astype(bf16)
    d_first = against(d_qkv[...], qkv_weight_ref[...])
    normed = hat_one[...]
    grad_gain_one = jnp.sum(d_first * normed, axis=0, keepdims=True)
    grad_shift_one = jnp.sum(d_first, axis=0, keepdims=True)
    back = norm_back(d_first, normed, inv_one, gain_one)
    lay_out(d_resid[...].astype(f32) + back, grad_inputs_ref, slice(CH, 2 * CH))

    for h in range(HEADS):
        for a in range(WIN):
            score_rows[h * WIN : (h + 1) * WIN, a * CELLS : (a + 1) * CELLS] = score_total[
                a * WIN : (a + 1) * WIN, h * CELLS : (h + 1) * CELLS
            ]
    table_mid[...] = split_dot(score_rows[...], pick_one_ref[...])
    strips = [table_mid[pl.ds(b, HEADS, stride=WIN), :] for b in range(WIN)]
    table = split_dot(jnp.concatenate(strips, axis=1), pick_two_ref[...])
    small = jnp.concatenate(
        [table, grad_gain_one, grad_shift_one, grad_gain_two, grad_shift_two, jnp.zeros((4, CH), f32)],
        axis=0,
    )
    packed[AT_SMALL : AT_SMALL + SMALL, :] = (small * scale).astype(bf16)
    rest = PACK_ROWS - AT_SMALL - SMALL
    packed[AT_SMALL + SMALL : PACK_ROWS, :] = jnp.zeros((rest, CH), bf16)
    keep_ref[...] = packed[pl.ds(pl.multiple_of(core * CORE_ROWS, 16), CORE_ROWS), :]
    give_ref[...] = packed[pl.ds(pl.multiple_of((1 - core) * CORE_ROWS, 16), CORE_ROWS), :]


def cut_kernel(inputs_ref, cotangent_ref, rows_ref, cols_ref, edge_ref, sems):
    last = pl.ds(COLS - 16, 16)
    copies = []
    for n, own_ref in enumerate((inputs_ref, cotangent_ref)):
        lanes = pl.ds(n * CH, CH)
        low = own_ref.at[pl.ds(HALF, HALF)]
        copies.append((low, rows_ref.at[:, :, lanes]))
        copies.append((own_ref.at[pl.ds(0, HALF), last], cols_ref.at[:, :, lanes]))
        copies.append((own_ref.at[pl.ds(HALF, HALF), last], edge_ref.at[:, :, lanes]))
    running = [
        pltpu.make_async_copy(source, target, sems.at[n])
        for n, (source, target) in enumerate(copies)
    ]
    for copy in running:
        copy.start()
    for copy in running:
        copy.wait()


def exact_parts(values):
    high = values.astype(bf16)
    rest = values - high.astype(f32)
    mid = rest.astype(bf16)
    return high, mid, (rest - mid.astype(f32)).astype(bf16)


def prepare_kernel(
    place_ref,
    valid_ref,
    table_ref,
    usable_ref,
    bias_ref,
    pick_one_ref,
    pick_two_ref,
    cells,
    table,
    mid,
    rows,
    sems,
):
    lat = place_ref[0]
    lon = place_ref[2]
    above = pl.multiple_of(lax.rem(lat * ROWS + NLAT - ROWS, NLAT), ROWS)
    own = pl.multiple_of(lat * ROWS, ROWS)
    copies = [
        pltpu.make_async_copy(valid_ref.at[pl.ds(above, ROWS)], cells.at[pl.ds(0, ROWS)], sems.at[0]),
        pltpu.make_async_copy(valid_ref.at[pl.ds(own, ROWS)], cells.at[pl.ds(ROWS, ROWS)], sems.at[1]),
    ]
    for copy in copies:
        copy.start()

    def iota(dims, axis):
        return lax.broadcasted_iota(jnp.int32, dims, axis)

    def as_low(choice):
        return jnp.where(choice, 1.0, 0.0).astype(bf16)

    dims = (PAIRS, 128)
    row, lane = iota(dims, 0), iota(dims, 1)
    pick_one = as_low((row // WIN % WIN - row // CELLS + WIN - 1) * WIN + row % WIN == lane)
    pick_one_ref[...] = pick_one
    dims = (WIN * 128, CH)
    row, lane = iota(dims, 0), iota(dims, 1)
    step = row // WIN % 16
    place = step * (2 * WIN - 1) + row % WIN - row // 128 + WIN - 1
    pick_two = as_low((place == lane) & (step < 2 * WIN - 1))
    pick_two_ref[...] = pick_two

    table[...] = jnp.zeros_like(table)
    table[:, 0:ENTRIES] = table_ref[...]
    spread = sum(against(part, pick_two) for part in exact_parts(table[...]))
    for b in range(WIN):
        mid[pl.ds(b, HEADS, stride=WIN), :] = spread[:, b * 128 : (b + 1) * 128]
    rows[...] = sum(against(part, pick_one) for part in exact_parts(mid[...]))
    for h in range(HEADS):
        for a in range(WIN):
            bias_ref[a * WIN : (a + 1) * WIN, h * CELLS : (h + 1) * CELLS] = rows[
                h * WIN : (h + 1) * WIN, a * CELLS : (a + 1) * CELLS
            ]

    for copy in copies:
        copy.wait()
    band = jnp.where(cells[HALF : HALF + ROWS, :] > 0, 1.0, 0.0).astype(bf16)
    dims = (NLON, 128)
    wanted = lax.rem(iota(dims, 1) + lon * COLS + NLON - HALF, NLON)
    line = dot(band, as_low(iota(dims, 0) == wanted))
    tall = jnp.concatenate(
        [jnp.broadcast_to(line[a : a + 1], (WIN, 128)) for a in range(WIN)], axis=0
    )
    dims = (CELLS, 128)
    row, lane = iota(dims, 0), iota(dims, 1)
    ones = jnp.ones((128, 128), bf16)
    for w in range(WINDOWS):
        chosen = jnp.where(lane == w * WIN + row % WIN, tall, 0.0).astype(bf16)
        usable_ref[w * CELLS : (w + 1) * CELLS, :] = dot(chosen, ones)


def finish_kernel(
    place_ref,
    mine_ref,
    other_ref,
    out_in_ref,
    grad_in_ref,
    below_ref,
    side_ref,
    edge_ref,
    output_ref,
    grad_inputs_ref,
    grad_qkv_ref,
    grad_proj_ref,
    grad_up_ref,
    grad_down_ref,
    gain_one_ref,
    shift_one_ref,
    gain_two_ref,
    shift_two_ref,
    table_ref,
    whole,
    wide,
):
    core = place_ref[1]
    whole[pl.ds(pl.multiple_of(core * CORE_ROWS, 16), CORE_ROWS), :] = mine_ref[...]
    whole[pl.ds(pl.multiple_of((1 - core) * CORE_ROWS, 16), CORE_ROWS), :] = other_ref[...]
    grad_down_ref[...] = whole[0:MLP, :].astype(f32)
    for k in range(MLP // CH):
        low = AT_UP + k * CH
        grad_up_ref[:, k * CH : (k + 1) * CH] = whole[low : low + CH, :].astype(f32)
    for k in range(3):
        low = AT_QKV + k * CH
        grad_qkv_ref[:, k * CH : (k + 1) * CH] = whole[low : low + CH, :].astype(f32)
    grad_proj_ref[...] = whole[AT_PROJ : AT_PROJ + CH, :].astype(f32)
    small = whole[AT_SMALL : AT_SMALL + SMALL, :].astype(f32)
    table_ref[...] = small[0:HEADS, 0:ENTRIES]
    gain_one_ref[...] = small[HEADS : HEADS + 1]
    shift_one_ref[...] = small[HEADS + 1 : HEADS + 2]
    gain_two_ref[...] = small[HEADS + 2 : HEADS + 3]
    shift_two_ref[...] = small[HEADS + 3 : HEADS + 4]
    for own_ref, out_ref, lanes in (
        (out_in_ref, output_ref, slice(0, CH)),
        (grad_in_ref, grad_inputs_ref, slice(CH, 2 * CH)),
    ):
        for a in range(ROWS):
            if a < HALF:
                wide[0:COLS, :] = own_ref[a + HALF].astype(f32)
                wide[COLS : COLS + 16, :] = side_ref[a, :, lanes].astype(f32)
            else:
                wide[0:COLS, :] = below_ref[a - HALF, :, lanes].astype(f32)
                wide[COLS : COLS + 16, :] = edge_ref[a - HALF, :, lanes].astype(f32)
            out_ref[a] = wide[HALF : HALF + COLS, :].astype(bf16)


def in_vmem():
    return pl.BlockSpec(memory_space=pltpu.VMEM)


def in_smem():
    return pl.BlockSpec(memory_space=pltpu.SMEM)


def shape(dims, dtype):
    return jax.ShapeDtypeStruct(dims, dtype)


def in_any():
    return pl.BlockSpec(memory_space=pl.ANY)


def run_cut(inputs, cotangent):
    return pl.pallas_call(
        cut_kernel,
        out_shape=(
            shape((HALF, COLS, 2 * CH), bf16),
            shape((HALF, 16, 2 * CH), bf16),
            shape((HALF, 16, 2 * CH), bf16),
        ),
        in_specs=[in_any()] * 2,
        out_specs=[in_vmem()] * 3,
        scratch_shapes=[pltpu.SemaphoreType.DMA((6,))],
        compiler_params=pltpu.CompilerParams(vmem_limit_bytes=56 * 1024 * 1024),
        cost_estimate=pl.CostEstimate(flops=1000, bytes_accessed=1_000_000, transcendentals=0),
    )(inputs, cotangent)


def run_prepare(place, valid_cells, bias_table):
    return pl.pallas_call(
        prepare_kernel,
        out_shape=(
            shape((LOCAL, 128), f32),
            shape((CELLS, PAIRS), f32),
            shape((PAIRS, 128), bf16),
            shape((WIN * 128, CH), bf16),
        ),
        in_specs=[in_smem(), in_any(), in_vmem()],
        out_specs=[in_vmem()] * 4,
        scratch_shapes=[
            pltpu.VMEM((2 * ROWS, NLON), jnp.int32),
            pltpu.VMEM((HEADS, CH), f32),
            pltpu.VMEM((CELLS, 128), f32),
            pltpu.VMEM((CELLS, PAIRS), f32),
            pltpu.SemaphoreType.DMA((2,)),
        ],
        compiler_params=pltpu.CompilerParams(vmem_limit_bytes=56 * 1024 * 1024),
        cost_estimate=pl.CostEstimate(
            flops=1_000_000_000, bytes_accessed=4_000_000, transcendentals=0
        ),
    )(place, valid_cells, bias_table)


def run_block(*operands):
    return pl.pallas_call(
        block_kernel,
        out_shape=(
            shape((ROWS, COLS, CH), bf16),
            shape((ROWS, COLS, CH), bf16),
            shape((HALF, COLS, 2 * CH), bf16),
            shape((HALF, 16, 2 * CH), bf16),
            shape((HALF, 16, 2 * CH), bf16),
            shape((CORE_ROWS, CH), bf16),
            shape((CORE_ROWS, CH), bf16),
        ),
        in_specs=[in_smem()] + [in_vmem()] * (len(operands) - 1),
        out_specs=[in_vmem()] * 7,
        scratch_shapes=[
            pltpu.VMEM((COLS + 16, CH), f32),
            pltpu.VMEM((LOCAL, CH), f32),
            pltpu.VMEM((LOCAL, CH), bf16),
            pltpu.VMEM((LOCAL, CH), f32),
            pltpu.VMEM((LOCAL, CH), bf16),
            pltpu.VMEM((LOCAL, 3 * CH), bf16),
            pltpu.VMEM((LOCAL, PAIRS), f32),
            pltpu.VMEM((LOCAL, CH), bf16),
            pltpu.VMEM((LOCAL, CH), bf16),
            pltpu.VMEM((LOCAL, CH), f32),
            pltpu.VMEM((LOCAL, CH), f32),
            pltpu.VMEM((LOCAL, CH), bf16),
            pltpu.VMEM((LOCAL, CH), bf16),
            pltpu.VMEM((LOCAL, 3 * CH), bf16),
            pltpu.VMEM((PAIRS, CH), bf16),
            pltpu.VMEM((CELLS, PAIRS), f32),
            pltpu.VMEM((CELLS, PAIRS), f32),
            pltpu.VMEM((CELLS, 128), f32),
            pltpu.VMEM((PACK_ROWS, CH), bf16),
        ],
        compiler_params=pltpu.CompilerParams(vmem_limit_bytes=48 * 1024 * 1024),
        cost_estimate=pl.CostEstimate(
            flops=4_000_000_000, bytes_accessed=8_000_000, transcendentals=2_000_000
        ),
    )(*operands)


def run_finish(*operands):
    return pl.pallas_call(
        finish_kernel,
        out_shape=(
            shape((ROWS, COLS, CH), bf16),
            shape((ROWS, COLS, CH), bf16),
            shape((CH, 3 * CH), f32),
            shape((CH, CH), f32),
            shape((CH, MLP), f32),
            shape((MLP, CH), f32),
            shape((1, CH), f32),
            shape((1, CH), f32),
            shape((1, CH), f32),
            shape((1, CH), f32),
            shape((HEADS, ENTRIES), f32),
        ),
        in_specs=[in_smem()] + [in_vmem()] * (len(operands) - 1),
        out_specs=[in_vmem()] * 11,
        scratch_shapes=[
            pltpu.VMEM((PACK_ROWS, CH), bf16),
            pltpu.VMEM((COLS + 16, CH), f32),
        ],
        compiler_params=pltpu.CompilerParams(vmem_limit_bytes=32 * 1024 * 1024),
        cost_estimate=pl.CostEstimate(flops=1_000_000, bytes_accessed=8_000_000, transcendentals=0),
    )(*operands)


def total_over_chips(keep, give, beside):
    swap = [(0, 1), (1, 0)]
    pair = keep.astype(f32) + lax.ppermute(give, "c", swap).astype(f32)
    pieces = pair.astype(bf16).reshape(PLANE_SIZE, PIECE, CH)
    pieces = lax.all_to_all(pieces, PLANE, 0, 0, tiled=True)
    pieces, beside = lax.optimization_barrier((pieces, beside))
    part = jnp.sum(pieces.astype(f32), axis=0).astype(bf16)
    depth = lax.axis_size("z")
    copies = jnp.broadcast_to(part[None], (depth, PIECE, CH))
    copies = lax.all_to_all(copies, "z", 0, 0, tiled=True)
    part = jnp.sum(copies.astype(f32), axis=0).astype(bf16)
    copies = jnp.broadcast_to(part[None], (PLANE_SIZE, PIECE, CH))
    mine = lax.all_to_all(copies, PLANE, 0, 0, tiled=True).reshape(CORE_ROWS, CH)
    return mine, lax.ppermute(mine, "c", swap), beside


def per_device(
    inputs,
    cotangent,
    valid_cells,
    gain_one,
    shift_one,
    gain_two,
    shift_two,
    qkv_weight,
    proj_weight,
    up_weight,
    down_weight,
    bias_table,
):
    place = jnp.stack(
        [lax.axis_index(LAT), lax.axis_index("c"), lax.axis_index(LON)]
    ).astype(jnp.int32)
    low_rows, top_last, low_last = run_cut(inputs, cotangent)
    above = moved(low_rows, 1, 0)
    beside = moved(top_last, 0, 1)
    corner = moved(low_last, 1, 1)
    usable, bias, pick_one, pick_two = run_prepare(place, valid_cells, bias_table)
    output, grad_inputs, below, side, edge, keep, give = run_block(
        place,
        inputs,
        cotangent,
        above,
        beside,
        corner,
        usable,
        gain_one.reshape(1, CH),
        shift_one.reshape(1, CH),
        gain_two.reshape(1, CH),
        shift_two.reshape(1, CH),
        qkv_weight,
        proj_weight,
        up_weight,
        down_weight,
        bias,
        pick_one,
        pick_two,
    )
    back = (moved(below, -1, 0), moved(side, 0, -1), moved(edge, -1, -1))
    mine, other, (below, side, edge) = total_over_chips(keep, give, back)
    found = run_finish(place, mine, other, output, grad_inputs, below, side, edge)
    return tuple(
        item.reshape(CH) if item.shape == (1, CH) else item for item in found
    )


def solution(mesh):
    split = jax.sharding.Mesh(mesh.devices.reshape(2, 4, 2, 2, 8), EVERY)
    field = P(LAT, LON, None)
    return jax.shard_map(
        per_device,
        mesh=split,
        in_specs=(field, field) + (P(),) * 10,
        out_specs=(field, field) + (P(),) * 9,
        check_vma=False,
    )
```

```python
import math

import jax
import jax.numpy as jnp
from jax import lax
from jax.experimental import pallas as pl
from jax.experimental.pallas import tpu as pltpu
from jax.sharding import PartitionSpec as P

WIN = 8
CELLS = WIN * WIN
HALF = WIN // 2
CH = 256
HEADS = 8
HEAD_DIM = 32
MLP = 1024
NLAT = 128
NLON = 1024
ROWS = 8
COLS = 64
WINDOWS = COLS // WIN
LOCAL = ROWS * COLS
PAIRS = HEADS * CELLS
ENTRIES = (2 * WIN - 1) * (2 * WIN - 1)

EPSILON = 1e-05
ROOT_HALF = 0.7071067811865476
INV_ROOT_TAU = 0.3989422804014327
NEVER = -1e30

LAT = ("xl", "y", "c")
LON = ("xh", "z")
EVERY = LAT + LON
PLANE = ("xl", "y", "xh")
SIDE = 16

AT_UP = MLP
AT_QKV = 2 * MLP
AT_PROJ = 2 * MLP + 3 * CH
AT_SMALL = 3 * MLP
SMALL = 16
PIECE = 104
PLANE_SIZE = 16
CORE_ROWS = PIECE * PLANE_SIZE
PACK_ROWS = 2 * CORE_ROWS

f32 = jnp.float32
bf16 = jnp.bfloat16


def moved(block, lat_step, lon_step):
    pairs = []
    for lat in range(SIDE):
        for lon in range(SIDE):
            target = ((lat + lat_step) % SIDE) * SIDE + (lon + lon_step) % SIDE
            pairs.append((lat * SIDE + lon, target))
    return lax.ppermute(block, EVERY, pairs)


def coordinates():
    lat = (lax.axis_index("xl") * 4 + lax.axis_index("y")) * 2 + lax.axis_index("c")
    return lat, lax.axis_index("xh") * 8 + lax.axis_index("z"), lax.axis_index("c")


def dot(left, right):
    return jnp.dot(left, right, preferred_element_type=f32)


def across(left, right):
    return lax.dot_general(left, right, (((0,), (0,)), ((), ())), preferred_element_type=f32)


def against(left, right):
    return lax.dot_general(left, right, (((1,), (1,)), ((), ())), preferred_element_type=f32)


def split_dot(left, right):
    high = left.astype(bf16)
    low = (left - high.astype(f32)).astype(bf16)
    return dot(high, right) + dot(low, right)


def row_stats(values):
    centred = values - jnp.mean(values, axis=-1, keepdims=True)
    inv_std = lax.rsqrt(jnp.mean(centred * centred, axis=-1, keepdims=True) + EPSILON)
    return centred * inv_std, inv_std


def norm_back(upstream, normed, inv_std, gain_vec):
    scaled = upstream * gain_vec
    return inv_std * (
        scaled
        - jnp.mean(scaled, axis=-1, keepdims=True)
        - normed * jnp.mean(scaled * normed, axis=-1, keepdims=True)
    )


def block_kernel(
    inputs_ref,
    cotangent_ref,
    above_ref,
    beside_ref,
    corner_ref,
    valid_ref,
    gain_one_ref,
    shift_one_ref,
    gain_two_ref,
    shift_two_ref,
    qkv_weight_ref,
    proj_weight_ref,
    up_weight_ref,
    down_weight_ref,
    bias_ref,
    output_ref,
    grad_inputs_ref,
    below_ref,
    side_ref,
    edge_ref,
    keep_ref,
    give_ref,
    wide,
    tokens,
    upstream,
    hat_one,
    first_in,
    qkv,
    probs,
    mixed,
    second_in,
    total_out,
    total_back,
    d_resid,
    d_mixed,
    d_qkv,
    head_rows,
    score_total,
    score_rows,
    table_mid,
    packed,
    d_scores,
    low,
):
    scale = 1.0 / math.sqrt(LOCAL * SIDE * SIDE)
    factor = HEAD_DIM**-0.5
    lat, _, core = coordinates()

    def assemble(own_ref, lanes, target):
        for a in range(ROWS):
            if a < HALF:
                wide[0:16, :] = corner_ref[a, :, lanes].astype(f32)
                wide[16 : 16 + COLS, :] = above_ref[a, :, lanes].astype(f32)
            else:
                wide[0:16, :] = beside_ref[a - HALF, :, lanes].astype(f32)
                wide[16 : 16 + COLS, :] = own_ref[a - HALF].astype(f32)
            line = wide[16 - HALF : 16 - HALF + COLS, :]
            for w in range(WINDOWS):
                target[w * CELLS + a * WIN : w * CELLS + (a + 1) * WIN, :] = line[
                    w * WIN : (w + 1) * WIN
                ].astype(target.dtype)

    assemble(inputs_ref, slice(0, CH), tokens)
    assemble(cotangent_ref, slice(CH, 2 * CH), total_back)
    upstream[...] = total_back[...].astype(bf16)

    lane_head = lax.broadcasted_iota(jnp.int32, (PAIRS // 2, 128), 1) // HEAD_DIM
    row_head = lax.broadcasted_iota(jnp.int32, (PAIRS // 2, 128), 0) // CELLS
    head_rows[...] = jnp.where(lane_head == row_head, 1.0, 0.0).astype(bf16)

    gain_one = gain_one_ref[...]
    normed, inv_one = row_stats(tokens[...])
    hat_one[...] = normed
    first = (normed * gain_one + shift_one_ref[...]).astype(bf16)
    first_in[...] = first
    qkv[...] = dot(first, qkv_weight_ref[...]).astype(bf16)

    halves = ((slice(0, 128), slice(0, PAIRS // 2)), (slice(128, CH), slice(PAIRS // 2, PAIRS)))
    lane_id = lax.broadcasted_iota(jnp.int32, (1, 128), 1)

    def spread(block):
        return [
            jnp.concatenate([block[:, lanes]] * (HEADS // 2), axis=0) * head_rows[...]
            for lanes, _ in halves
        ]

    def per_pair(block, spread_block):
        return jnp.concatenate(
            [against(block[:, lanes], half) for (lanes, _), half in zip(halves, spread_block)],
            axis=1,
        )

    def per_key(block, spread_block):
        return jnp.concatenate(
            [dot(block[:, pairs], half) for (_, pairs), half in zip(halves, spread_block)],
            axis=1,
        )

    def per_query(block, values):
        sides = []
        for lanes, pairs in halves:
            full = across(block[:, pairs], values[:, lanes])
            side = full[0:CELLS]
            for h in range(1, HEADS // 2):
                part = full[h * CELLS : (h + 1) * CELLS]
                side = jnp.where(lane_id >= h * HEAD_DIM, part, side)
            sides.append(side)
        return jnp.concatenate(sides, axis=1)

    key_id = lax.broadcasted_iota(jnp.int32, (CELLS, PAIRS), 0)
    query_id = lax.rem(lax.broadcasted_iota(jnp.int32, (CELLS, PAIRS), 1), CELLS)
    same_cell = key_id == query_id
    same_side = ((key_id < CELLS // 2) == (query_id < CELLS // 2)) | (lat > 0)

    def window(w):
        return slice(w * CELLS, (w + 1) * CELLS)

    for w in range(WINDOWS):
        rows = window(w)
        scores = per_pair(qkv[rows, CH : 2 * CH], spread(qkv[rows, 0:CH]))
        probs[rows, :] = scores * factor + bias_ref[...]
    for w in range(WINDOWS):
        rows = window(w)
        usable = jnp.broadcast_to(valid_ref[:, w : w + 1], (CELLS, PAIRS)) > 0.0
        scores = jnp.where((usable | same_cell) & same_side, probs[rows, :], NEVER)
        weights = jnp.exp(scores - jnp.max(scores, axis=0, keepdims=True))
        probs[rows, :] = weights * (1.0 / jnp.sum(weights, axis=0, keepdims=True))
    for w in range(WINDOWS):
        rows = window(w)
        values_in = qkv[rows, 2 * CH : 3 * CH]
        mixed[rows, :] = per_query(probs[rows, :].astype(bf16), values_in).astype(bf16)

    resid = (tokens[...] + dot(mixed[...], proj_weight_ref[...])).astype(bf16).astype(f32)
    hat_two, inv_two = row_stats(resid)
    gain_two = gain_two_ref[...]
    second_in[...] = (hat_two * gain_two + shift_two_ref[...]).astype(bf16)
    total_out[...] = resid
    total_back[...] = jnp.zeros_like(total_back)

    def feed(k):
        cols = slice(k * CH, (k + 1) * CH)
        up_part = up_weight_ref[:, cols]
        down_part = down_weight_ref[cols, :]
        second = second_in[...]
        grads = upstream[...]
        raised = dot(second, up_part)
        area = 0.5 * (1.0 + lax.erf(raised * ROOT_HALF))
        hidden = (raised * area).astype(bf16)
        slope = area + raised * jnp.exp(-0.5 * raised * raised) * INV_ROOT_TAU
        d_raised = (against(grads, down_part) * slope).astype(bf16)
        total_out[...] += dot(hidden, down_part)
        total_back[...] += against(d_raised, up_part)
        packed[cols, :] = (across(hidden, grads) * scale).astype(bf16)
        packed[AT_UP + k * CH : AT_UP + (k + 1) * CH, :] = (
            across(second, d_raised) * scale
        ).astype(bf16)

    for k in range(MLP // CH):
        feed(k)

    def lay_out(values, out_ref, lanes):
        for a in range(ROWS):
            line = jnp.concatenate(
                [
                    values[w * CELLS + a * WIN : w * CELLS + (a + 1) * WIN]
                    for w in range(WINDOWS)
                ],
                axis=0,
            ).astype(bf16)
            out_ref[a] = line
            if a < HALF:
                below_ref[a, :, lanes] = line
                edge_ref[a, :, lanes] = line[:16]
            else:
                side_ref[a - HALF, :, lanes] = line[:16]

    lay_out(total_out[...], output_ref, slice(0, CH))

    d_second = total_back[...]
    grad_gain_two = jnp.sum(d_second * hat_two, axis=0, keepdims=True)
    grad_shift_two = jnp.sum(d_second, axis=0, keepdims=True)
    back = norm_back(d_second, hat_two, inv_two, gain_two)
    d_low = (upstream[...].astype(f32) + back).astype(bf16)
    d_resid[...] = d_low
    packed[AT_PROJ : AT_PROJ + CH, :] = (across(mixed[...], d_low) * scale).astype(bf16)
    d_mixed[...] = against(d_low, proj_weight_ref[...]).astype(bf16)
    score_total[...] = jnp.zeros_like(score_total)

    for w in range(WINDOWS):
        rows = window(w)
        d_scores[rows, :] = per_pair(qkv[rows, 2 * CH : 3 * CH], spread(d_mixed[rows, :]))
    for w in range(WINDOWS):
        rows = window(w)
        share = probs[rows, :]
        d_share = d_scores[rows, :]
        back_scores = share * (d_share - jnp.sum(share * d_share, axis=0, keepdims=True))
        score_total[...] += back_scores
        low[rows, :] = back_scores.astype(bf16)
    for w in range(WINDOWS):
        rows = window(w)
        grads = spread(d_mixed[rows, :])
        queries = spread(qkv[rows, 0:CH])
        keys_in = qkv[rows, CH : 2 * CH]
        low_part = low[rows, :]
        d_qkv[rows, 0:CH] = (per_query(low_part, keys_in) * factor).astype(bf16)
        d_qkv[rows, CH : 2 * CH] = (per_key(low_part, queries) * factor).astype(bf16)
        d_qkv[rows, 2 * CH : 3 * CH] = per_key(probs[rows, :].astype(bf16), grads).astype(bf16)

    for part in range(3):
        lanes = slice(part * CH, (part + 1) * CH)
        found = across(first_in[...], d_qkv[:, lanes]) * scale
        packed[AT_QKV + part * CH : AT_QKV + (part + 1) * CH, :] = found.astype(bf16)
    d_first = against(d_qkv[...], qkv_weight_ref[...])
    normed = hat_one[...]
    grad_gain_one = jnp.sum(d_first * normed, axis=0, keepdims=True)
    grad_shift_one = jnp.sum(d_first, axis=0, keepdims=True)
    back = norm_back(d_first, normed, inv_one, gain_one)
    lay_out(d_resid[...].astype(f32) + back, grad_inputs_ref, slice(CH, 2 * CH))

    for h in range(HEADS):
        for a in range(WIN):
            score_rows[h * WIN : (h + 1) * WIN, a * CELLS : (a + 1) * CELLS] = score_total[
                a * WIN : (a + 1) * WIN, h * CELLS : (h + 1) * CELLS
            ]
    table_mid[...] = split_dot(score_rows[...], pick_step())
    strips = [table_mid[pl.ds(b, HEADS, stride=WIN), :] for b in range(WIN)]
    table = split_dot(jnp.concatenate(strips, axis=1), pick_entry())
    small = jnp.concatenate(
        [table, grad_gain_one, grad_shift_one, grad_gain_two, grad_shift_two, jnp.zeros((4, CH), f32)],
        axis=0,
    )
    packed[AT_SMALL : AT_SMALL + SMALL, :] = (small * scale).astype(bf16)
    rest = PACK_ROWS - AT_SMALL - SMALL
    packed[AT_SMALL + SMALL : PACK_ROWS, :] = jnp.zeros((rest, CH), bf16)
    keep_ref[...] = packed[pl.ds(pl.multiple_of(core * CORE_ROWS, 16), CORE_ROWS), :]
    give_ref[...] = packed[pl.ds(pl.multiple_of((1 - core) * CORE_ROWS, 16), CORE_ROWS), :]


def iota(dims, axis):
    return lax.broadcasted_iota(jnp.int32, dims, axis)


def as_low(choice):
    return jnp.where(choice, 1.0, 0.0).astype(bf16)


def pick_step():
    row = iota((PAIRS, 1), 0)
    wanted = (row // WIN % WIN - row // CELLS + WIN - 1) * WIN + row % WIN
    return as_low(wanted == iota((PAIRS, 128), 1))


def pick_entry():
    row = iota((WIN * 128, 1), 0)
    step = row // WIN % 16
    place = step * (2 * WIN - 1) + row % WIN - row // 128 + WIN - 1
    wanted = jnp.where(step < 2 * WIN - 1, place, -1)
    return as_low(wanted == iota((WIN * 128, CH), 1))


def exact_parts(values):
    high = values.astype(bf16)
    rest = values - high.astype(f32)
    mid = rest.astype(bf16)
    return high, mid, (rest - mid.astype(f32)).astype(bf16)


def cut_kernel(inputs_ref, cotangent_ref, rows_ref, cols_ref, edge_ref, sems):
    last = pl.ds(COLS - 16, 16)
    pairs = []
    for n, own_ref in enumerate((inputs_ref, cotangent_ref)):
        lanes = pl.ds(n * CH, CH)
        pairs.append((own_ref.at[pl.ds(HALF, HALF)], rows_ref.at[:, :, lanes]))
        pairs.append((own_ref.at[pl.ds(0, HALF), last], cols_ref.at[:, :, lanes]))
        pairs.append((own_ref.at[pl.ds(HALF, HALF), last], edge_ref.at[:, :, lanes]))
    copies = [
        pltpu.make_async_copy(source, target, sems.at[n])
        for n, (source, target) in enumerate(pairs)
    ]
    for copy in copies:
        copy.start()
    for copy in copies:
        copy.wait()


def prepare_kernel(
    valid_ref,
    table_ref,
    usable_ref,
    bias_ref,
    cells,
    table,
    mid,
    rows,
    sems,
):
    lat, lon, _ = coordinates()
    pairs = []
    above = pl.multiple_of(lax.rem(lat * ROWS + NLAT - ROWS, NLAT), ROWS)
    own = pl.multiple_of(lat * ROWS, ROWS)
    pairs.append((valid_ref.at[pl.ds(above, ROWS)], cells.at[pl.ds(0, ROWS)]))
    pairs.append((valid_ref.at[pl.ds(own, ROWS)], cells.at[pl.ds(ROWS, ROWS)]))
    copies = [
        pltpu.make_async_copy(source, target, sems.at[n])
        for n, (source, target) in enumerate(pairs)
    ]
    for copy in copies:
        copy.start()

    pick_one, pick_two = pick_step(), pick_entry()
    dims = (NLON, 128)
    wanted = lax.rem(iota((1, 128), 1) + lon * COLS + NLON - HALF, NLON)
    pick_cols = as_low(iota(dims, 0) == wanted)
    table[...] = jnp.zeros_like(table)
    table[:, 0:ENTRIES] = table_ref[...]
    spread = sum(against(part, pick_two) for part in exact_parts(table[...]))
    for b in range(WIN):
        mid[pl.ds(b, HEADS, stride=WIN), :] = spread[:, b * 128 : (b + 1) * 128]
    rows[...] = sum(against(part, pick_one) for part in exact_parts(mid[...]))
    for h in range(HEADS):
        for a in range(WIN):
            bias_ref[a * WIN : (a + 1) * WIN, h * CELLS : (h + 1) * CELLS] = rows[
                h * WIN : (h + 1) * WIN, a * CELLS : (a + 1) * CELLS
            ]

    for copy in copies:
        copy.wait()
    band = jnp.where(cells[HALF : HALF + ROWS, :] > 0, 1.0, 0.0).astype(bf16)
    line = dot(band, pick_cols)
    tall = jnp.concatenate(
        [jnp.broadcast_to(line[a : a + 1], (WIN, 128)) for a in range(WIN)], axis=0
    )
    row, lane = iota((CELLS, 128), 0), iota((CELLS, 128), 1)
    chosen = jnp.where((lane % WIN == row % WIN) & (lane < COLS), tall, 0.0).astype(bf16)
    window = as_low(iota((128, 128), 0) // WIN == iota((128, 128), 1))
    usable_ref[...] = dot(chosen, window)


def fields_kernel(
    out_in_ref, grad_in_ref, below_ref, side_ref, edge_ref, output_ref, grad_inputs_ref, wide
):
    for own_ref, out_ref, lanes in (
        (out_in_ref, output_ref, slice(0, CH)),
        (grad_in_ref, grad_inputs_ref, slice(CH, 2 * CH)),
    ):
        for a in range(ROWS):
            if a < HALF:
                wide[0:COLS, :] = own_ref[a + HALF].astype(f32)
                wide[COLS : COLS + 16, :] = side_ref[a, :, lanes].astype(f32)
            else:
                wide[0:COLS, :] = below_ref[a - HALF, :, lanes].astype(f32)
                wide[COLS : COLS + 16, :] = edge_ref[a - HALF, :, lanes].astype(f32)
            out_ref[a] = wide[HALF : HALF + COLS, :].astype(bf16)


def grads_kernel(
    mine_ref,
    other_ref,
    grad_qkv_ref,
    grad_proj_ref,
    grad_up_ref,
    grad_down_ref,
    gain_one_ref,
    shift_one_ref,
    gain_two_ref,
    shift_two_ref,
    table_ref,
    qkv,
    proj,
    up,
    down,
    sems,
):
    _, _, core = coordinates()
    first = core == 0
    copies = []

    def rows_at(low, count):
        half, at = divmod(low, CORE_ROWS)
        mine = mine_ref[at : at + count, :]
        other = other_ref[at : at + count, :]
        return jnp.where(first == (half == 0), mine, other).astype(f32)

    def send(source, target):
        copies.append(pltpu.make_async_copy(source, target, sems.at[len(copies)]))
        copies[-1].start()

    for low in range(0, MLP, CH):
        rows = pl.ds(low, CH)
        down[rows, :] = rows_at(low, CH)
        send(down.at[rows], grad_down_ref.at[rows])
    for k in range(MLP // CH):
        cols = pl.ds(k * CH, CH)
        for part in range(2):
            rows = slice(part * 128, (part + 1) * 128)
            up[rows, k * CH : (k + 1) * CH] = rows_at(AT_UP + k * CH + part * 128, 128)
        send(up.at[:, cols], grad_up_ref.at[:, cols])
    for k in range(3):
        cols = pl.ds(k * CH, CH)
        qkv[:, k * CH : (k + 1) * CH] = rows_at(AT_QKV + k * CH, CH)
        send(qkv.at[:, cols], grad_qkv_ref.at[:, cols])
    proj[...] = rows_at(AT_PROJ, CH)
    send(proj, grad_proj_ref)
    small = rows_at(AT_SMALL, SMALL)
    table_ref[...] = small[0:HEADS, 0:ENTRIES]
    gain_one_ref[...] = small[HEADS : HEADS + 1]
    shift_one_ref[...] = small[HEADS + 1 : HEADS + 2]
    gain_two_ref[...] = small[HEADS + 2 : HEADS + 3]
    shift_two_ref[...] = small[HEADS + 3 : HEADS + 4]
    for copy in copies:
        copy.wait()


def in_vmem():
    return pl.BlockSpec(memory_space=pltpu.VMEM)


def shape(dims, dtype):
    return jax.ShapeDtypeStruct(dims, dtype)


def in_any():
    return pl.BlockSpec(memory_space=pl.ANY)


def run_cut(inputs, cotangent):
    return pl.pallas_call(
        cut_kernel,
        out_shape=(
            shape((HALF, COLS, 2 * CH), bf16),
            shape((HALF, 16, 2 * CH), bf16),
            shape((HALF, 16, 2 * CH), bf16),
        ),
        in_specs=[in_any()] * 2,
        out_specs=[in_vmem()] * 3,
        scratch_shapes=[pltpu.SemaphoreType.DMA((6,))],
        compiler_params=pltpu.CompilerParams(vmem_limit_bytes=8 * 1024 * 1024),
        cost_estimate=pl.CostEstimate(flops=1000, bytes_accessed=1_000_000, transcendentals=0),
    )(inputs, cotangent)


def run_prepare(valid_cells, bias_table):
    return pl.pallas_call(
        prepare_kernel,
        out_shape=(shape((CELLS, 128), f32), shape((CELLS, PAIRS), f32)),
        in_specs=[in_any(), in_vmem()],
        out_specs=[in_vmem()] * 2,
        scratch_shapes=[
            pltpu.VMEM((2 * ROWS, NLON), jnp.int32),
            pltpu.VMEM((HEADS, CH), f32),
            pltpu.VMEM((CELLS, 128), f32),
            pltpu.VMEM((CELLS, PAIRS), f32),
            pltpu.SemaphoreType.DMA((2,)),
        ],
        compiler_params=pltpu.CompilerParams(vmem_limit_bytes=8 * 1024 * 1024),
        cost_estimate=pl.CostEstimate(
            flops=500_000_000, bytes_accessed=2_000_000, transcendentals=0
        ),
    )(valid_cells, bias_table)


def run_block(*operands):
    return pl.pallas_call(
        block_kernel,
        out_shape=(
            shape((ROWS, COLS, CH), bf16),
            shape((ROWS, COLS, CH), bf16),
            shape((HALF, COLS, 2 * CH), bf16),
            shape((HALF, 16, 2 * CH), bf16),
            shape((HALF, 16, 2 * CH), bf16),
            shape((CORE_ROWS, CH), bf16),
            shape((CORE_ROWS, CH), bf16),
        ),
        in_specs=[in_vmem()] * len(operands),
        out_specs=[in_vmem()] * 7,
        scratch_shapes=[
            pltpu.VMEM((COLS + 16, CH), f32),
            pltpu.VMEM((LOCAL, CH), f32),
            pltpu.VMEM((LOCAL, CH), bf16),
            pltpu.VMEM((LOCAL, CH), f32),
            pltpu.VMEM((LOCAL, CH), bf16),
            pltpu.VMEM((LOCAL, 3 * CH), bf16),
            pltpu.VMEM((LOCAL, PAIRS), f32),
            pltpu.VMEM((LOCAL, CH), bf16),
            pltpu.VMEM((LOCAL, CH), bf16),
            pltpu.VMEM((LOCAL, CH), f32),
            pltpu.VMEM((LOCAL, CH), f32),
            pltpu.VMEM((LOCAL, CH), bf16),
            pltpu.VMEM((LOCAL, CH), bf16),
            pltpu.VMEM((LOCAL, 3 * CH), bf16),
            pltpu.VMEM((PAIRS // 2, 128), bf16),
            pltpu.VMEM((CELLS, PAIRS), f32),
            pltpu.VMEM((CELLS, PAIRS), f32),
            pltpu.VMEM((CELLS, 128), f32),
            pltpu.VMEM((PACK_ROWS, CH), bf16),
            pltpu.VMEM((LOCAL, PAIRS), f32),
            pltpu.VMEM((LOCAL, PAIRS), bf16),
        ],
        compiler_params=pltpu.CompilerParams(vmem_limit_bytes=32 * 1024 * 1024),
        cost_estimate=pl.CostEstimate(
            flops=4_000_000_000, bytes_accessed=8_000_000, transcendentals=2_000_000
        ),
    )(*operands)


def run_fields(*operands):
    return pl.pallas_call(
        fields_kernel,
        out_shape=(shape((ROWS, COLS, CH), bf16),) * 2,
        in_specs=[in_vmem()] * len(operands),
        out_specs=[in_vmem()] * 2,
        scratch_shapes=[pltpu.VMEM((COLS + 16, CH), f32)],
        compiler_params=pltpu.CompilerParams(vmem_limit_bytes=16 * 1024 * 1024),
        cost_estimate=pl.CostEstimate(flops=1_000_000, bytes_accessed=2_000_000, transcendentals=0),
    )(*operands)


def run_grads(mine, other):
    return pl.pallas_call(
        grads_kernel,
        out_shape=(
            shape((CH, 3 * CH), f32),
            shape((CH, CH), f32),
            shape((CH, MLP), f32),
            shape((MLP, CH), f32),
            shape((1, CH), f32),
            shape((1, CH), f32),
            shape((1, CH), f32),
            shape((1, CH), f32),
            shape((HEADS, ENTRIES), f32),
        ),
        in_specs=[in_vmem()] * 2,
        out_specs=[in_any()] * 4 + [in_vmem()] * 5,
        scratch_shapes=[
            pltpu.VMEM((CH, 3 * CH), f32),
            pltpu.VMEM((CH, CH), f32),
            pltpu.VMEM((CH, MLP), f32),
            pltpu.VMEM((MLP, CH), f32),
            pltpu.SemaphoreType.DMA((12,)),
        ],
        compiler_params=pltpu.CompilerParams(vmem_limit_bytes=32 * 1024 * 1024),
        cost_estimate=pl.CostEstimate(flops=1_000_000, bytes_accessed=8_000_000, transcendentals=0),
    )(mine, other)


def total_over_chips(keep, give, beside):
    swap = [(0, 1), (1, 0)]
    pair = keep.astype(f32) + lax.ppermute(give, "c", swap).astype(f32)
    pieces = pair.astype(bf16).reshape(PLANE_SIZE, PIECE, CH)
    pieces = lax.all_to_all(pieces, PLANE, 0, 0, tiled=True)
    part = jnp.sum(pieces.astype(f32), axis=0).astype(bf16)
    depth = lax.axis_size("z")
    copies = jnp.broadcast_to(part[None], (depth, PIECE, CH))
    copies = lax.all_to_all(copies, "z", 0, 0, tiled=True)
    part = jnp.sum(copies.astype(f32), axis=0).astype(bf16)
    copies = jnp.broadcast_to(part[None], (PLANE_SIZE, PIECE, CH))
    mine = lax.all_to_all(copies, PLANE, 0, 0, tiled=True).reshape(CORE_ROWS, CH)
    return mine, lax.ppermute(mine, "c", swap), beside


def per_device(
    inputs,
    cotangent,
    valid_cells,
    gain_one,
    shift_one,
    gain_two,
    shift_two,
    qkv_weight,
    proj_weight,
    up_weight,
    down_weight,
    bias_table,
):
    low_rows, top_last, low_last = run_cut(inputs, cotangent)
    above = moved(low_rows, 1, 0)
    beside = moved(top_last, 0, 1)
    corner = moved(low_last, 1, 1)
    usable, bias = run_prepare(valid_cells, bias_table)
    output, grad_inputs, below, side, edge, keep, give = run_block(
        inputs,
        cotangent,
        above,
        beside,
        corner,
        usable,
        gain_one.reshape(1, CH),
        shift_one.reshape(1, CH),
        gain_two.reshape(1, CH),
        shift_two.reshape(1, CH),
        qkv_weight,
        proj_weight,
        up_weight,
        down_weight,
        bias,
    )
    back = (moved(below, -1, 0), moved(side, 0, -1), moved(edge, -1, -1))
    mine, other, (below, side, edge) = total_over_chips(keep, give, back)
    grads = run_grads(mine, other)
    table, (below, side, edge) = lax.optimization_barrier((grads[-1], (below, side, edge)))
    fields = run_fields(output, grad_inputs, below, side, edge)
    grads = grads[:-1] + (table,)
    return fields + tuple(
        item.reshape(CH) if item.shape == (1, CH) else item for item in grads
    )


def solution(mesh):
    split = jax.sharding.Mesh(mesh.devices.reshape(2, 4, 2, 2, 8), EVERY)
    field = P(LAT, LON, None)
    return jax.shard_map(
        per_device,
        mesh=split,
        in_specs=(field, field) + (P(),) * 10,
        out_specs=(field, field) + (P(),) * 9,
        check_vma=False,
    )
```

```python
import math

import jax
import jax.numpy as jnp
from jax import lax
from jax.experimental import pallas as pl
from jax.experimental.pallas import tpu as pltpu
from jax.sharding import PartitionSpec as P

WIN = 8
CELLS = WIN * WIN
HALF = WIN // 2
CH = 256
HEADS = 8
HEAD_DIM = 32
MLP = 1024
NLAT = 128
NLON = 1024
ROWS = 8
COLS = 64
WINDOWS = COLS // WIN
LOCAL = ROWS * COLS
PAIRS = HEADS * CELLS
ENTRIES = (2 * WIN - 1) * (2 * WIN - 1)

EPSILON = 1e-05
ROOT_HALF = 0.7071067811865476
INV_ROOT_TAU = 0.3989422804014327
NEVER = -1e30

LAT = ("xl", "y", "c")
LON = ("xh", "zh", "zl")
EVERY = LAT + LON
NEAR = ("xl", "y", "xh", "zl")
FAR = "zh"
SHAPE = (2, 4, 2, 2, 4, 2)
SIDE = 16

BLOCKS = 12
AT_UP = 4
AT_QKV = 8
AT_PROJ = 11
SMALL = 16
NEAR_SIZE = 32
FAR_SIZE = 4
PER_HALF = BLOCKS // 2
WIDTH = PER_HALF * CH + 128

f32 = jnp.float32
bf16 = jnp.bfloat16


def moved(block, lat_step, lon_step):
    pairs = []
    for lat in range(SIDE):
        for lon in range(SIDE):
            target = ((lat + lat_step) % SIDE) * SIDE + (lon + lon_step) % SIDE
            pairs.append((lat * SIDE + lon, target))
    return lax.ppermute(block, EVERY, pairs)


def coordinates():
    lat = (lax.axis_index("xl") * 4 + lax.axis_index("y")) * 2 + lax.axis_index("c")
    return lat, lax.axis_index("xh") * 8 + lax.axis_index("zh") * 2 + lax.axis_index("zl"), (
        lax.axis_index("c")
    )


def dot(left, right):
    return jnp.dot(left, right, preferred_element_type=f32)


def across(left, right):
    return lax.dot_general(left, right, (((0,), (0,)), ((), ())), preferred_element_type=f32)


def against(left, right):
    return lax.dot_general(left, right, (((1,), (1,)), ((), ())), preferred_element_type=f32)


def split_dot(left, right):
    high = left.astype(bf16)
    low = (left - high.astype(f32)).astype(bf16)
    return dot(high, right) + dot(low, right)


def row_stats(values):
    centred = values - jnp.mean(values, axis=-1, keepdims=True)
    inv_std = lax.rsqrt(jnp.mean(centred * centred, axis=-1, keepdims=True) + EPSILON)
    return centred * inv_std, inv_std


def norm_back(upstream, normed, inv_std, gain_vec):
    scaled = upstream * gain_vec
    return inv_std * (
        scaled
        - jnp.mean(scaled, axis=-1, keepdims=True)
        - normed * jnp.mean(scaled * normed, axis=-1, keepdims=True)
    )


def block_kernel(
    inputs_ref,
    cotangent_ref,
    above_ref,
    beside_ref,
    corner_ref,
    valid_ref,
    gain_one_ref,
    shift_one_ref,
    gain_two_ref,
    shift_two_ref,
    qkv_weight_ref,
    proj_weight_ref,
    up_weight_ref,
    down_weight_ref,
    bias_ref,
    output_ref,
    grad_inputs_ref,
    below_ref,
    side_ref,
    edge_ref,
    keep_ref,
    give_ref,
    wide,
    tokens,
    upstream,
    hat_one,
    first_in,
    qkv,
    probs,
    mixed,
    second_in,
    total_out,
    total_back,
    d_resid,
    d_mixed,
    d_qkv,
    head_rows,
    score_total,
    score_rows,
    table_mid,
    packed,
    d_scores,
    low,
):
    scale = 1.0 / math.sqrt(LOCAL * SIDE * SIDE)

    def pack(block, values):
        half, place = divmod(block, PER_HALF)
        packed[half, :, place * CH : (place + 1) * CH] = (values * scale).astype(bf16)

    factor = HEAD_DIM**-0.5
    lat, _, core = coordinates()

    def assemble(own_ref, lanes, target):
        for a in range(ROWS):
            if a < HALF:
                wide[0:16, :] = corner_ref[a, :, lanes].astype(f32)
                wide[16 : 16 + COLS, :] = above_ref[a, :, lanes].astype(f32)
            else:
                wide[0:16, :] = beside_ref[a - HALF, :, lanes].astype(f32)
                wide[16 : 16 + COLS, :] = own_ref[a - HALF].astype(f32)
            line = wide[16 - HALF : 16 - HALF + COLS, :]
            for w in range(WINDOWS):
                target[w * CELLS + a * WIN : w * CELLS + (a + 1) * WIN, :] = line[
                    w * WIN : (w + 1) * WIN
                ].astype(target.dtype)

    assemble(inputs_ref, slice(0, CH), tokens)
    assemble(cotangent_ref, slice(CH, 2 * CH), total_back)
    upstream[...] = total_back[...].astype(bf16)

    lane_head = lax.broadcasted_iota(jnp.int32, (PAIRS // 2, 128), 1) // HEAD_DIM
    row_head = lax.broadcasted_iota(jnp.int32, (PAIRS // 2, 128), 0) // CELLS
    head_rows[...] = jnp.where(lane_head == row_head, 1.0, 0.0).astype(bf16)

    gain_one = gain_one_ref[...]
    normed, inv_one = row_stats(tokens[...])
    hat_one[...] = normed
    first = (normed * gain_one + shift_one_ref[...]).astype(bf16)
    first_in[...] = first
    qkv[...] = dot(first, qkv_weight_ref[...]).astype(bf16)

    halves = ((slice(0, 128), slice(0, PAIRS // 2)), (slice(128, CH), slice(PAIRS // 2, PAIRS)))
    lane_id = lax.broadcasted_iota(jnp.int32, (1, 128), 1)

    def spread(block):
        return [
            jnp.concatenate([block[:, lanes]] * (HEADS // 2), axis=0) * head_rows[...]
            for lanes, _ in halves
        ]

    def per_pair(block, spread_block):
        return jnp.concatenate(
            [against(block[:, lanes], half) for (lanes, _), half in zip(halves, spread_block)],
            axis=1,
        )

    def per_key(block, spread_block):
        return jnp.concatenate(
            [dot(block[:, pairs], half) for (_, pairs), half in zip(halves, spread_block)],
            axis=1,
        )

    def per_query(block, values):
        sides = []
        for lanes, pairs in halves:
            full = across(block[:, pairs], values[:, lanes])
            side = full[0:CELLS]
            for h in range(1, HEADS // 2):
                part = full[h * CELLS : (h + 1) * CELLS]
                side = jnp.where(lane_id >= h * HEAD_DIM, part, side)
            sides.append(side)
        return jnp.concatenate(sides, axis=1)

    key_id = lax.broadcasted_iota(jnp.int32, (CELLS, PAIRS), 0)
    query_id = lax.rem(lax.broadcasted_iota(jnp.int32, (CELLS, PAIRS), 1), CELLS)
    same_cell = key_id == query_id
    same_side = ((key_id < CELLS // 2) == (query_id < CELLS // 2)) | (lat > 0)

    def window(w):
        return slice(w * CELLS, (w + 1) * CELLS)

    for w in range(WINDOWS):
        rows = window(w)
        scores = per_pair(qkv[rows, CH : 2 * CH], spread(qkv[rows, 0:CH]))
        probs[rows, :] = scores * factor + bias_ref[...]
    for w in range(WINDOWS):
        rows = window(w)
        usable = jnp.broadcast_to(valid_ref[:, w : w + 1], (CELLS, PAIRS)) > 0.0
        scores = jnp.where((usable | same_cell) & same_side, probs[rows, :], NEVER)
        weights = jnp.exp(scores - jnp.max(scores, axis=0, keepdims=True))
        probs[rows, :] = weights * (1.0 / jnp.sum(weights, axis=0, keepdims=True))
    for w in range(WINDOWS):
        rows = window(w)
        values_in = qkv[rows, 2 * CH : 3 * CH]
        mixed[rows, :] = per_query(probs[rows, :].astype(bf16), values_in).astype(bf16)

    resid = (tokens[...] + dot(mixed[...], proj_weight_ref[...])).astype(bf16).astype(f32)
    hat_two, inv_two = row_stats(resid)
    gain_two = gain_two_ref[...]
    second_in[...] = (hat_two * gain_two + shift_two_ref[...]).astype(bf16)
    total_out[...] = resid
    total_back[...] = jnp.zeros_like(total_back)

    def feed(k):
        cols = slice(k * CH, (k + 1) * CH)
        up_part = up_weight_ref[:, cols]
        down_part = down_weight_ref[cols, :]
        second = second_in[...]
        grads = upstream[...]
        raised = dot(second, up_part)
        area = 0.5 * (1.0 + lax.erf(raised * ROOT_HALF))
        hidden = (raised * area).astype(bf16)
        slope = area + raised * jnp.exp(-0.5 * raised * raised) * INV_ROOT_TAU
        d_raised = (against(grads, down_part) * slope).astype(bf16)
        total_out[...] += dot(hidden, down_part)
        total_back[...] += against(d_raised, up_part)
        pack(k, across(hidden, grads))
        pack(AT_UP + k, across(second, d_raised))

    for k in range(MLP // CH):
        feed(k)

    def lay_out(values, out_ref, lanes):
        for a in range(ROWS):
            line = jnp.concatenate(
                [
                    values[w * CELLS + a * WIN : w * CELLS + (a + 1) * WIN]
                    for w in range(WINDOWS)
                ],
                axis=0,
            ).astype(bf16)
            out_ref[a] = line
            if a < HALF:
                below_ref[a, :, lanes] = line
                edge_ref[a, :, lanes] = line[:16]
            else:
                side_ref[a - HALF, :, lanes] = line[:16]

    lay_out(total_out[...], output_ref, slice(0, CH))

    d_second = total_back[...]
    grad_gain_two = jnp.sum(d_second * hat_two, axis=0, keepdims=True)
    grad_shift_two = jnp.sum(d_second, axis=0, keepdims=True)
    back = norm_back(d_second, hat_two, inv_two, gain_two)
    d_low = (upstream[...].astype(f32) + back).astype(bf16)
    d_resid[...] = d_low
    pack(AT_PROJ, across(mixed[...], d_low))
    d_mixed[...] = against(d_low, proj_weight_ref[...]).astype(bf16)
    score_total[...] = jnp.zeros_like(score_total)

    for w in range(WINDOWS):
        rows = window(w)
        d_scores[rows, :] = per_pair(qkv[rows, 2 * CH : 3 * CH], spread(d_mixed[rows, :]))
    for w in range(WINDOWS):
        rows = window(w)
        share = probs[rows, :]
        d_share = d_scores[rows, :]
        back_scores = share * (d_share - jnp.sum(share * d_share, axis=0, keepdims=True))
        score_total[...] += back_scores
        low[rows, :] = back_scores.astype(bf16)
    for w in range(WINDOWS):
        rows = window(w)
        grads = spread(d_mixed[rows, :])
        queries = spread(qkv[rows, 0:CH])
        keys_in = qkv[rows, CH : 2 * CH]
        low_part = low[rows, :]
        d_qkv[rows, 0:CH] = (per_query(low_part, keys_in) * factor).astype(bf16)
        d_qkv[rows, CH : 2 * CH] = (per_key(low_part, queries) * factor).astype(bf16)
        d_qkv[rows, 2 * CH : 3 * CH] = per_key(probs[rows, :].astype(bf16), grads).astype(bf16)

    for part in range(3):
        lanes = slice(part * CH, (part + 1) * CH)
        pack(AT_QKV + part, across(first_in[...], d_qkv[:, lanes]))
    d_first = against(d_qkv[...], qkv_weight_ref[...])
    normed = hat_one[...]
    grad_gain_one = jnp.sum(d_first * normed, axis=0, keepdims=True)
    grad_shift_one = jnp.sum(d_first, axis=0, keepdims=True)
    back = norm_back(d_first, normed, inv_one, gain_one)
    lay_out(d_resid[...].astype(f32) + back, grad_inputs_ref, slice(CH, 2 * CH))

    for h in range(HEADS):
        for a in range(WIN):
            score_rows[h * WIN : (h + 1) * WIN, a * CELLS : (a + 1) * CELLS] = score_total[
                a * WIN : (a + 1) * WIN, h * CELLS : (h + 1) * CELLS
            ]
    table_mid[...] = split_dot(score_rows[...], pick_step())
    strips = [table_mid[pl.ds(b, HEADS, stride=WIN), :] for b in range(WIN)]
    table = split_dot(jnp.concatenate(strips, axis=1), pick_entry())
    small = jnp.concatenate(
        [table, grad_gain_one, grad_shift_one, grad_gain_two, grad_shift_two, jnp.zeros((4, CH), f32)],
        axis=0,
    )
    small = (small * scale).astype(bf16)
    side = slice(PER_HALF * CH, WIDTH)
    packed[0, 0:SMALL, side] = small[:, 0:128]
    packed[0, SMALL : 2 * SMALL, side] = small[:, 128:CH]
    packed[0, 2 * SMALL : CH, side] = jnp.zeros((CH - 2 * SMALL, 128), bf16)
    packed[1, :, side] = jnp.zeros((CH, 128), bf16)
    keep_ref[...] = packed[core]
    give_ref[...] = packed[1 - core]


def iota(dims, axis):
    return lax.broadcasted_iota(jnp.int32, dims, axis)


def as_low(choice):
    return jnp.where(choice, 1.0, 0.0).astype(bf16)


def pick_step():
    row = iota((PAIRS, 1), 0)
    wanted = (row // WIN % WIN - row // CELLS + WIN - 1) * WIN + row % WIN
    return as_low(wanted == iota((PAIRS, 128), 1))


def pick_entry():
    row = iota((WIN * 128, 1), 0)
    step = row // WIN % 16
    place = step * (2 * WIN - 1) + row % WIN - row // 128 + WIN - 1
    wanted = jnp.where(step < 2 * WIN - 1, place, -1)
    return as_low(wanted == iota((WIN * 128, CH), 1))


def exact_parts(values):
    high = values.astype(bf16)
    rest = values - high.astype(f32)
    mid = rest.astype(bf16)
    return high, mid, (rest - mid.astype(f32)).astype(bf16)


def cut_kernel(inputs_ref, cotangent_ref, rows_ref, cols_ref, edge_ref, sems):
    last = pl.ds(COLS - 16, 16)
    pairs = []
    for n, own_ref in enumerate((inputs_ref, cotangent_ref)):
        lanes = pl.ds(n * CH, CH)
        pairs.append((own_ref.at[pl.ds(HALF, HALF)], rows_ref.at[:, :, lanes]))
        pairs.append((own_ref.at[pl.ds(0, HALF), last], cols_ref.at[:, :, lanes]))
        pairs.append((own_ref.at[pl.ds(HALF, HALF), last], edge_ref.at[:, :, lanes]))
    copies = [
        pltpu.make_async_copy(source, target, sems.at[n])
        for n, (source, target) in enumerate(pairs)
    ]
    for copy in copies:
        copy.start()
    for copy in copies:
        copy.wait()


def prepare_kernel(
    valid_ref,
    table_ref,
    usable_ref,
    bias_ref,
    cells,
    table,
    mid,
    rows,
    sems,
):
    lat, lon, _ = coordinates()
    pairs = []
    above = pl.multiple_of(lax.rem(lat * ROWS + NLAT - ROWS, NLAT), ROWS)
    own = pl.multiple_of(lat * ROWS, ROWS)
    pairs.append((valid_ref.at[pl.ds(above, ROWS)], cells.at[pl.ds(0, ROWS)]))
    pairs.append((valid_ref.at[pl.ds(own, ROWS)], cells.at[pl.ds(ROWS, ROWS)]))
    copies = [
        pltpu.make_async_copy(source, target, sems.at[n])
        for n, (source, target) in enumerate(pairs)
    ]
    for copy in copies:
        copy.start()

    pick_one, pick_two = pick_step(), pick_entry()
    dims = (NLON, 128)
    wanted = lax.rem(iota((1, 128), 1) + lon * COLS + NLON - HALF, NLON)
    pick_cols = as_low(iota(dims, 0) == wanted)
    table[...] = jnp.zeros_like(table)
    table[:, 0:ENTRIES] = table_ref[...]
    spread = sum(against(part, pick_two) for part in exact_parts(table[...]))
    for b in range(WIN):
        mid[pl.ds(b, HEADS, stride=WIN), :] = spread[:, b * 128 : (b + 1) * 128]
    rows[...] = sum(against(part, pick_one) for part in exact_parts(mid[...]))
    for h in range(HEADS):
        for a in range(WIN):
            bias_ref[a * WIN : (a + 1) * WIN, h * CELLS : (h + 1) * CELLS] = rows[
                h * WIN : (h + 1) * WIN, a * CELLS : (a + 1) * CELLS
            ]

    for copy in copies:
        copy.wait()
    band = jnp.where(cells[HALF : HALF + ROWS, :] > 0, 1.0, 0.0).astype(bf16)
    line = dot(band, pick_cols)
    tall = jnp.concatenate(
        [jnp.broadcast_to(line[a : a + 1], (WIN, 128)) for a in range(WIN)], axis=0
    )
    row, lane = iota((CELLS, 128), 0), iota((CELLS, 128), 1)
    chosen = jnp.where((lane % WIN == row % WIN) & (lane < COLS), tall, 0.0).astype(bf16)
    window = as_low(iota((128, 128), 0) // WIN == iota((128, 128), 1))
    usable_ref[...] = dot(chosen, window)


def fields_kernel(
    out_in_ref, grad_in_ref, below_ref, side_ref, edge_ref, output_ref, grad_inputs_ref, wide
):
    for own_ref, out_ref, lanes in (
        (out_in_ref, output_ref, slice(0, CH)),
        (grad_in_ref, grad_inputs_ref, slice(CH, 2 * CH)),
    ):
        for a in range(ROWS):
            if a < HALF:
                wide[0:COLS, :] = own_ref[a + HALF].astype(f32)
                wide[COLS : COLS + 16, :] = side_ref[a, :, lanes].astype(f32)
            else:
                wide[0:COLS, :] = below_ref[a - HALF, :, lanes].astype(f32)
                wide[COLS : COLS + 16, :] = edge_ref[a - HALF, :, lanes].astype(f32)
            out_ref[a] = wide[HALF : HALF + COLS, :].astype(bf16)


def grads_kernel(
    mine_ref,
    other_ref,
    grad_qkv_ref,
    grad_proj_ref,
    grad_up_ref,
    grad_down_ref,
    gain_one_ref,
    shift_one_ref,
    gain_two_ref,
    shift_two_ref,
    table_ref,
    qkv,
    proj,
    up,
    down,
    sems,
):
    _, _, core = coordinates()
    first = core == 0
    copies = []

    def found(half, rows, lanes):
        mine, other = mine_ref[rows, lanes], other_ref[rows, lanes]
        return jnp.where(first == (half == 0), mine, other).astype(f32)

    def block(number, rows):
        half, place = divmod(number, PER_HALF)
        return found(half, rows, slice(place * CH, (place + 1) * CH))

    def send(source, target):
        copies.append(pltpu.make_async_copy(source, target, sems.at[len(copies)]))
        copies[-1].start()

    for k in range(MLP // CH):
        down[k * CH : (k + 1) * CH, :] = block(k, slice(0, CH))
        rows = pl.ds(k * CH, CH)
        send(down.at[rows], grad_down_ref.at[rows])
    for wide, target, at, count in (
        (up, grad_up_ref, AT_UP, MLP // CH),
        (qkv, grad_qkv_ref, AT_QKV, 3),
    ):
        for low in range(0, CH, 128):
            for k in range(count):
                wide[low : low + 128, k * CH : (k + 1) * CH] = block(
                    at + k, slice(low, low + 128)
                )
            send(wide.at[pl.ds(low, 128)], target.at[pl.ds(low, 128)])
    proj[...] = block(AT_PROJ, slice(0, CH))
    send(proj, grad_proj_ref)
    side = slice(PER_HALF * CH, WIDTH)
    small = jnp.concatenate(
        [found(0, slice(0, SMALL), side), found(0, slice(SMALL, 2 * SMALL), side)], axis=1
    )
    table_ref[...] = small[0:HEADS, 0:ENTRIES]
    gain_one_ref[...] = small[HEADS : HEADS + 1]
    shift_one_ref[...] = small[HEADS + 1 : HEADS + 2]
    gain_two_ref[...] = small[HEADS + 2 : HEADS + 3]
    shift_two_ref[...] = small[HEADS + 3 : HEADS + 4]
    for copy in copies:
        copy.wait()


def in_vmem():
    return pl.BlockSpec(memory_space=pltpu.VMEM)


def shape(dims, dtype):
    return jax.ShapeDtypeStruct(dims, dtype)


def in_any():
    return pl.BlockSpec(memory_space=pl.ANY)


def run_cut(inputs, cotangent):
    return pl.pallas_call(
        cut_kernel,
        out_shape=(
            shape((HALF, COLS, 2 * CH), bf16),
            shape((HALF, 16, 2 * CH), bf16),
            shape((HALF, 16, 2 * CH), bf16),
        ),
        in_specs=[in_any()] * 2,
        out_specs=[in_vmem()] * 3,
        scratch_shapes=[pltpu.SemaphoreType.DMA((6,))],
        compiler_params=pltpu.CompilerParams(vmem_limit_bytes=8 * 1024 * 1024),
        cost_estimate=pl.CostEstimate(flops=1000, bytes_accessed=1_000_000, transcendentals=0),
    )(inputs, cotangent)


def run_prepare(valid_cells, bias_table):
    return pl.pallas_call(
        prepare_kernel,
        out_shape=(shape((CELLS, 128), f32), shape((CELLS, PAIRS), f32)),
        in_specs=[in_any(), in_vmem()],
        out_specs=[in_vmem()] * 2,
        scratch_shapes=[
            pltpu.VMEM((2 * ROWS, NLON), jnp.int32),
            pltpu.VMEM((HEADS, CH), f32),
            pltpu.VMEM((CELLS, 128), f32),
            pltpu.VMEM((CELLS, PAIRS), f32),
            pltpu.SemaphoreType.DMA((2,)),
        ],
        compiler_params=pltpu.CompilerParams(vmem_limit_bytes=8 * 1024 * 1024),
        cost_estimate=pl.CostEstimate(
            flops=500_000_000, bytes_accessed=2_000_000, transcendentals=0
        ),
    )(valid_cells, bias_table)


def run_block(*operands):
    return pl.pallas_call(
        block_kernel,
        out_shape=(
            shape((ROWS, COLS, CH), bf16),
            shape((ROWS, COLS, CH), bf16),
            shape((HALF, COLS, 2 * CH), bf16),
            shape((HALF, 16, 2 * CH), bf16),
            shape((HALF, 16, 2 * CH), bf16),
            shape((CH, WIDTH), bf16),
            shape((CH, WIDTH), bf16),
        ),
        in_specs=[in_vmem()] * len(operands),
        out_specs=[in_vmem()] * 7,
        scratch_shapes=[
            pltpu.VMEM((COLS + 16, CH), f32),
            pltpu.VMEM((LOCAL, CH), f32),
            pltpu.VMEM((LOCAL, CH), bf16),
            pltpu.VMEM((LOCAL, CH), f32),
            pltpu.VMEM((LOCAL, CH), bf16),
            pltpu.VMEM((LOCAL, 3 * CH), bf16),
            pltpu.VMEM((LOCAL, PAIRS), f32),
            pltpu.VMEM((LOCAL, CH), bf16),
            pltpu.VMEM((LOCAL, CH), bf16),
            pltpu.VMEM((LOCAL, CH), f32),
            pltpu.VMEM((LOCAL, CH), f32),
            pltpu.VMEM((LOCAL, CH), bf16),
            pltpu.VMEM((LOCAL, CH), bf16),
            pltpu.VMEM((LOCAL, 3 * CH), bf16),
            pltpu.VMEM((PAIRS // 2, 128), bf16),
            pltpu.VMEM((CELLS, PAIRS), f32),
            pltpu.VMEM((CELLS, PAIRS), f32),
            pltpu.VMEM((CELLS, 128), f32),
            pltpu.VMEM((2, CH, WIDTH), bf16),
            pltpu.VMEM((LOCAL, PAIRS), f32),
            pltpu.VMEM((LOCAL, PAIRS), bf16),
        ],
        compiler_params=pltpu.CompilerParams(vmem_limit_bytes=32 * 1024 * 1024),
        cost_estimate=pl.CostEstimate(
            flops=4_000_000_000, bytes_accessed=8_000_000, transcendentals=2_000_000
        ),
    )(*operands)


def run_fields(*operands):
    return pl.pallas_call(
        fields_kernel,
        out_shape=(shape((ROWS, COLS, CH), bf16),) * 2,
        in_specs=[in_vmem()] * len(operands),
        out_specs=[in_vmem()] * 2,
        scratch_shapes=[pltpu.VMEM((COLS + 16, CH), f32)],
        compiler_params=pltpu.CompilerParams(vmem_limit_bytes=16 * 1024 * 1024),
        cost_estimate=pl.CostEstimate(flops=1_000_000, bytes_accessed=2_000_000, transcendentals=0),
    )(*operands)


def run_grads(mine, other):
    return pl.pallas_call(
        grads_kernel,
        out_shape=(
            shape((CH, 3 * CH), f32),
            shape((CH, CH), f32),
            shape((CH, MLP), f32),
            shape((MLP, CH), f32),
            shape((1, CH), f32),
            shape((1, CH), f32),
            shape((1, CH), f32),
            shape((1, CH), f32),
            shape((HEADS, ENTRIES), f32),
        ),
        in_specs=[in_vmem()] * 2,
        out_specs=[in_any()] * 4 + [in_vmem()] * 5,
        scratch_shapes=[
            pltpu.VMEM((CH, 3 * CH), f32),
            pltpu.VMEM((CH, CH), f32),
            pltpu.VMEM((CH, MLP), f32),
            pltpu.VMEM((MLP, CH), f32),
            pltpu.SemaphoreType.DMA((12,)),
        ],
        compiler_params=pltpu.CompilerParams(vmem_limit_bytes=32 * 1024 * 1024),
        cost_estimate=pl.CostEstimate(flops=1_000_000, bytes_accessed=8_000_000, transcendentals=0),
    )(mine, other)


def total_over_chips(keep, give, beside):
    swap = [(0, 1), (1, 0)]
    pair = keep.astype(f32) + lax.ppermute(give, "c", swap).astype(f32)
    rows = CH // NEAR_SIZE
    pieces = pair.astype(bf16).reshape(NEAR_SIZE, rows, WIDTH)
    pieces = lax.all_to_all(pieces, NEAR, 0, 0, tiled=True)
    part = jnp.sum(pieces.astype(f32), axis=0).astype(bf16)
    copies = jnp.broadcast_to(part[None], (FAR_SIZE, rows, WIDTH))
    copies = lax.all_to_all(copies, FAR, 0, 0, tiled=True)
    part = jnp.sum(copies.astype(f32), axis=0).astype(bf16)
    copies = jnp.broadcast_to(part[None], (NEAR_SIZE, rows, WIDTH))
    mine = lax.all_to_all(copies, NEAR, 0, 0, tiled=True).reshape(CH, WIDTH)
    return mine, lax.ppermute(mine, "c", swap), beside


def per_device(
    inputs,
    cotangent,
    valid_cells,
    gain_one,
    shift_one,
    gain_two,
    shift_two,
    qkv_weight,
    proj_weight,
    up_weight,
    down_weight,
    bias_table,
):
    low_rows, top_last, low_last = run_cut(inputs, cotangent)
    above = moved(low_rows, 1, 0)
    beside = moved(top_last, 0, 1)
    corner = moved(low_last, 1, 1)
    usable, bias = run_prepare(valid_cells, bias_table)
    output, grad_inputs, below, side, edge, keep, give = run_block(
        inputs,
        cotangent,
        above,
        beside,
        corner,
        usable,
        gain_one.reshape(1, CH),
        shift_one.reshape(1, CH),
        gain_two.reshape(1, CH),
        shift_two.reshape(1, CH),
        qkv_weight,
        proj_weight,
        up_weight,
        down_weight,
        bias,
    )
    back = (moved(below, -1, 0), moved(side, 0, -1), moved(edge, -1, -1))
    mine, other, (below, side, edge) = total_over_chips(keep, give, back)
    grads = run_grads(mine, other)
    table, (below, side, edge) = lax.optimization_barrier((grads[-1], (below, side, edge)))
    fields = run_fields(output, grad_inputs, below, side, edge)
    grads = grads[:-1] + (table,)
    return fields + tuple(
        item.reshape(CH) if item.shape == (1, CH) else item for item in grads
    )


def solution(mesh):
    split = jax.sharding.Mesh(mesh.devices.reshape(SHAPE), EVERY)
    field = P(LAT, LON, None)
    return jax.shard_map(
        per_device,
        mesh=split,
        in_specs=(field, field) + (P(),) * 10,
        out_specs=(field, field) + (P(),) * 9,
        check_vma=False,
    )
```

```python
import math

import jax
import jax.numpy as jnp
from jax import lax
from jax.experimental import pallas as pl
from jax.experimental.pallas import tpu as pltpu
from jax.sharding import PartitionSpec as P

WIN = 8
CELLS = WIN * WIN
HALF = WIN // 2
CH = 256
HEADS = 8
HEAD_DIM = 32
MLP = 1024
NLAT = 128
NLON = 1024
ROWS = 8
COLS = 64
WINDOWS = COLS // WIN
LOCAL = ROWS * COLS
PAIRS = HEADS * CELLS
ENTRIES = (2 * WIN - 1) * (2 * WIN - 1)

EPSILON = 1e-05
ROOT_HALF = 0.7071067811865476
INV_ROOT_TAU = 0.3989422804014327
NEVER = -1e30

LAT = ("xl", "y", "c")
LON = ("xh", "zh", "zl")
EVERY = LAT + LON
NEAR = ("xl", "y", "xh", "zl")
FAR = "zh"
SHAPE = (2, 4, 2, 2, 4, 2)
SIDE = 16

BLOCKS = 12
AT_UP = 4
AT_QKV = 8
AT_PROJ = 11
SMALL = 16
NEAR_SIZE = 32
FAR_SIZE = 4
PER_HALF = BLOCKS // 2
WIDTH = PER_HALF * CH + 128

f32 = jnp.float32
bf16 = jnp.bfloat16


def moved(block, lat_step, lon_step):
    pairs = []
    for lat in range(SIDE):
        for lon in range(SIDE):
            target = ((lat + lat_step) % SIDE) * SIDE + (lon + lon_step) % SIDE
            pairs.append((lat * SIDE + lon, target))
    return lax.ppermute(block, EVERY, pairs)


def coordinates():
    lat = (lax.axis_index("xl") * 4 + lax.axis_index("y")) * 2 + lax.axis_index("c")
    return lat, lax.axis_index("xh") * 8 + lax.axis_index("zh") * 2 + lax.axis_index("zl"), (
        lax.axis_index("c")
    )


def dot(left, right):
    return jnp.dot(left, right, preferred_element_type=f32)


def across(left, right):
    return lax.dot_general(left, right, (((0,), (0,)), ((), ())), preferred_element_type=f32)


def against(left, right):
    return lax.dot_general(left, right, (((1,), (1,)), ((), ())), preferred_element_type=f32)


def split_dot(left, right):
    high = left.astype(bf16)
    low = (left - high.astype(f32)).astype(bf16)
    return dot(high, right) + dot(low, right)


def row_stats(values):
    centred = values - jnp.mean(values, axis=-1, keepdims=True)
    inv_std = lax.rsqrt(jnp.mean(centred * centred, axis=-1, keepdims=True) + EPSILON)
    return centred * inv_std, inv_std


def norm_back(upstream, normed, inv_std, gain_vec):
    scaled = upstream * gain_vec
    return inv_std * (
        scaled
        - jnp.mean(scaled, axis=-1, keepdims=True)
        - normed * jnp.mean(scaled * normed, axis=-1, keepdims=True)
    )


def block_kernel(
    inputs_ref,
    cotangent_ref,
    above_ref,
    beside_ref,
    corner_ref,
    valid_ref,
    gain_one_ref,
    shift_one_ref,
    gain_two_ref,
    shift_two_ref,
    qkv_weight_ref,
    proj_weight_ref,
    up_weight_ref,
    down_weight_ref,
    bias_ref,
    output_ref,
    grad_inputs_ref,
    below_ref,
    side_ref,
    edge_ref,
    keep_ref,
    give_ref,
    wide,
    tokens,
    upstream,
    hat_one,
    first_in,
    qkv,
    probs,
    mixed,
    second_in,
    total_out,
    total_back,
    d_resid,
    d_mixed,
    d_qkv,
    head_rows,
    score_total,
    score_rows,
    table_mid,
    packed,
    d_scores,
    low,
    strip,
):
    scale = 1.0 / math.sqrt(LOCAL * SIDE * SIDE)

    def pack(block, values):
        half, place = divmod(block, PER_HALF)
        packed[half, :, place * CH : (place + 1) * CH] = (values * scale).astype(bf16)

    factor = HEAD_DIM**-0.5
    lat, _, core = coordinates()

    def assemble(own_ref, lanes, target):
        strip[0:16, :] = corner_ref[:, lanes].astype(f32)
        strip[16:32, :] = beside_ref[:, lanes].astype(f32)
        for a in range(ROWS):
            wide[16 - HALF : 16, :] = strip[a * HALF : (a + 1) * HALF, :]
            if a < HALF:
                wide[16 : 16 + COLS, :] = above_ref[a, :, lanes].astype(f32)
            else:
                wide[16 : 16 + COLS, :] = own_ref[a - HALF].astype(f32)
            line = wide[16 - HALF : 16 - HALF + COLS, :]
            for w in range(WINDOWS):
                target[w * CELLS + a * WIN : w * CELLS + (a + 1) * WIN, :] = line[
                    w * WIN : (w + 1) * WIN
                ].astype(target.dtype)

    assemble(inputs_ref, slice(0, CH), tokens)
    assemble(cotangent_ref, slice(CH, 2 * CH), total_back)
    upstream[...] = total_back[...].astype(bf16)

    lane_head = lax.broadcasted_iota(jnp.int32, (PAIRS // 2, 128), 1) // HEAD_DIM
    row_head = lax.broadcasted_iota(jnp.int32, (PAIRS // 2, 128), 0) // CELLS
    head_rows[...] = jnp.where(lane_head == row_head, 1.0, 0.0).astype(bf16)

    gain_one = gain_one_ref[...]
    normed, inv_one = row_stats(tokens[...])
    hat_one[...] = normed
    first = (normed * gain_one + shift_one_ref[...]).astype(bf16)
    first_in[...] = first
    qkv[...] = dot(first, qkv_weight_ref[...]).astype(bf16)

    halves = ((slice(0, 128), slice(0, PAIRS // 2)), (slice(128, CH), slice(PAIRS // 2, PAIRS)))
    lane_id = lax.broadcasted_iota(jnp.int32, (1, 128), 1)

    def spread(block):
        return [
            jnp.concatenate([block[:, lanes]] * (HEADS // 2), axis=0) * head_rows[...]
            for lanes, _ in halves
        ]

    def per_pair(block, spread_block):
        return jnp.concatenate(
            [against(block[:, lanes], half) for (lanes, _), half in zip(halves, spread_block)],
            axis=1,
        )

    def per_key(block, spread_block):
        return jnp.concatenate(
            [dot(block[:, pairs], half) for (_, pairs), half in zip(halves, spread_block)],
            axis=1,
        )

    def per_query(block, values):
        sides = []
        for lanes, pairs in halves:
            full = across(block[:, pairs], values[:, lanes])
            side = full[0:CELLS]
            for h in range(1, HEADS // 2):
                part = full[h * CELLS : (h + 1) * CELLS]
                side = jnp.where(lane_id >= h * HEAD_DIM, part, side)
            sides.append(side)
        return jnp.concatenate(sides, axis=1)

    key_id = lax.broadcasted_iota(jnp.int32, (CELLS, PAIRS), 0)
    query_id = lax.rem(lax.broadcasted_iota(jnp.int32, (CELLS, PAIRS), 1), CELLS)
    same_cell = key_id == query_id
    same_side = ((key_id < CELLS // 2) == (query_id < CELLS // 2)) | (lat > 0)

    def window(w):
        return slice(w * CELLS, (w + 1) * CELLS)

    for w in range(WINDOWS):
        rows = window(w)
        scores = per_pair(qkv[rows, CH : 2 * CH], spread(qkv[rows, 0:CH]))
        probs[rows, :] = scores * factor + bias_ref[...]
    for w in range(WINDOWS):
        rows = window(w)
        usable = jnp.broadcast_to(valid_ref[:, w : w + 1], (CELLS, PAIRS)) > 0.0
        scores = jnp.where((usable | same_cell) & same_side, probs[rows, :], NEVER)
        weights = jnp.exp(scores - jnp.max(scores, axis=0, keepdims=True))
        probs[rows, :] = weights * (1.0 / jnp.sum(weights, axis=0, keepdims=True))
    for w in range(WINDOWS):
        rows = window(w)
        values_in = qkv[rows, 2 * CH : 3 * CH]
        mixed[rows, :] = per_query(probs[rows, :].astype(bf16), values_in).astype(bf16)

    resid = (tokens[...] + dot(mixed[...], proj_weight_ref[...])).astype(bf16).astype(f32)
    hat_two, inv_two = row_stats(resid)
    gain_two = gain_two_ref[...]
    second_in[...] = (hat_two * gain_two + shift_two_ref[...]).astype(bf16)
    total_out[...] = resid
    total_back[...] = jnp.zeros_like(total_back)

    def feed(k):
        cols = slice(k * CH, (k + 1) * CH)
        up_part = up_weight_ref[:, cols]
        down_part = down_weight_ref[cols, :]
        second = second_in[...]
        grads = upstream[...]
        raised = dot(second, up_part)
        area = 0.5 * (1.0 + lax.erf(raised * ROOT_HALF))
        hidden = (raised * area).astype(bf16)
        slope = area + raised * jnp.exp(-0.5 * raised * raised) * INV_ROOT_TAU
        d_raised = (against(grads, down_part) * slope).astype(bf16)
        total_out[...] += dot(hidden, down_part)
        total_back[...] += against(d_raised, up_part)
        pack(k, across(hidden, grads))
        pack(AT_UP + k, across(second, d_raised))

    for k in range(MLP // CH):
        feed(k)

    def lay_out(values, out_ref, lanes):
        for a in range(ROWS):
            line = jnp.concatenate(
                [
                    values[w * CELLS + a * WIN : w * CELLS + (a + 1) * WIN]
                    for w in range(WINDOWS)
                ],
                axis=0,
            )
            strip[a * HALF : (a + 1) * HALF, :] = line[0:HALF]
            out_ref[a] = line.astype(bf16)
            if a < HALF:
                below_ref[a, :, lanes] = line.astype(bf16)
        edge_ref[:, lanes] = strip[0:16, :].astype(bf16)
        side_ref[:, lanes] = strip[16:32, :].astype(bf16)

    lay_out(total_out[...], output_ref, slice(0, CH))

    d_second = total_back[...]
    grad_gain_two = jnp.sum(d_second * hat_two, axis=0, keepdims=True)
    grad_shift_two = jnp.sum(d_second, axis=0, keepdims=True)
    back = norm_back(d_second, hat_two, inv_two, gain_two)
    d_low = (upstream[...].astype(f32) + back).astype(bf16)
    d_resid[...] = d_low
    pack(AT_PROJ, across(mixed[...], d_low))
    d_mixed[...] = against(d_low, proj_weight_ref[...]).astype(bf16)
    score_total[...] = jnp.zeros_like(score_total)

    for w in range(WINDOWS):
        rows = window(w)
        d_scores[rows, :] = per_pair(qkv[rows, 2 * CH : 3 * CH], spread(d_mixed[rows, :]))
    for w in range(WINDOWS):
        rows = window(w)
        share = probs[rows, :]
        d_share = d_scores[rows, :]
        back_scores = share * (d_share - jnp.sum(share * d_share, axis=0, keepdims=True))
        score_total[...] += back_scores
        low[rows, :] = back_scores.astype(bf16)
    for w in range(WINDOWS):
        rows = window(w)
        grads = spread(d_mixed[rows, :])
        queries = spread(qkv[rows, 0:CH])
        keys_in = qkv[rows, CH : 2 * CH]
        low_part = low[rows, :]
        d_qkv[rows, 0:CH] = (per_query(low_part, keys_in) * factor).astype(bf16)
        d_qkv[rows, CH : 2 * CH] = (per_key(low_part, queries) * factor).astype(bf16)
        d_qkv[rows, 2 * CH : 3 * CH] = per_key(probs[rows, :].astype(bf16), grads).astype(bf16)

    for part in range(3):
        lanes = slice(part * CH, (part + 1) * CH)
        pack(AT_QKV + part, across(first_in[...], d_qkv[:, lanes]))
    d_first = against(d_qkv[...], qkv_weight_ref[...])
    normed = hat_one[...]
    grad_gain_one = jnp.sum(d_first * normed, axis=0, keepdims=True)
    grad_shift_one = jnp.sum(d_first, axis=0, keepdims=True)
    back = norm_back(d_first, normed, inv_one, gain_one)
    lay_out(d_resid[...].astype(f32) + back, grad_inputs_ref, slice(CH, 2 * CH))

    for h in range(HEADS):
        for a in range(WIN):
            score_rows[h * WIN : (h + 1) * WIN, a * CELLS : (a + 1) * CELLS] = score_total[
                a * WIN : (a + 1) * WIN, h * CELLS : (h + 1) * CELLS
            ]
    table_mid[...] = split_dot(score_rows[...], pick_step())
    strips = [table_mid[pl.ds(b, HEADS, stride=WIN), :] for b in range(WIN)]
    table = split_dot(jnp.concatenate(strips, axis=1), pick_entry())
    small = jnp.concatenate(
        [table, grad_gain_one, grad_shift_one, grad_gain_two, grad_shift_two, jnp.zeros((4, CH), f32)],
        axis=0,
    )
    small = (small * scale).astype(bf16)
    side = slice(PER_HALF * CH, WIDTH)
    packed[0, 0:SMALL, side] = small[:, 0:128]
    packed[0, SMALL : 2 * SMALL, side] = small[:, 128:CH]
    packed[0, 2 * SMALL : CH, side] = jnp.zeros((CH - 2 * SMALL, 128), bf16)
    packed[1, :, side] = jnp.zeros((CH, 128), bf16)
    keep_ref[...] = packed[core]
    give_ref[...] = packed[1 - core]


def iota(dims, axis):
    return lax.broadcasted_iota(jnp.int32, dims, axis)


def as_low(choice):
    return jnp.where(choice, 1.0, 0.0).astype(bf16)


def pick_step():
    row = iota((PAIRS, 1), 0)
    wanted = (row // WIN % WIN - row // CELLS + WIN - 1) * WIN + row % WIN
    return as_low(wanted == iota((PAIRS, 128), 1))


def pick_entry():
    row = iota((WIN * 128, 1), 0)
    step = row // WIN % 16
    place = step * (2 * WIN - 1) + row % WIN - row // 128 + WIN - 1
    wanted = jnp.where(step < 2 * WIN - 1, place, -1)
    return as_low(wanted == iota((WIN * 128, CH), 1))


def exact_parts(values):
    high = values.astype(bf16)
    rest = values - high.astype(f32)
    mid = rest.astype(bf16)
    return high, mid, (rest - mid.astype(f32)).astype(bf16)


def cut_kernel(
    inputs_ref, cotangent_ref, rows_ref, cols_ref, edge_ref, grabbed, wide, strip, sems
):
    pairs = []
    for n, own_ref in enumerate((inputs_ref, cotangent_ref)):
        pairs.append((own_ref.at[:, pl.ds(COLS - 16, 16)], grabbed.at[n]))
    for n, own_ref in enumerate((inputs_ref, cotangent_ref)):
        pairs.append((own_ref.at[pl.ds(HALF, HALF)], rows_ref.at[:, :, pl.ds(n * CH, CH)]))
    copies = [
        pltpu.make_async_copy(source, target, sems.at[n])
        for n, (source, target) in enumerate(pairs)
    ]
    for copy in copies:
        copy.start()
    for n in range(2):
        copies[n].wait()
        lanes = slice(n * CH, (n + 1) * CH)
        for a in range(ROWS):
            wide[...] = grabbed[n, a].astype(f32)
            strip[a * HALF : (a + 1) * HALF, :] = wide[16 - HALF : 16, :]
        cols_ref[:, lanes] = strip[0:16, :].astype(bf16)
        edge_ref[:, lanes] = strip[16:32, :].astype(bf16)
    for copy in copies[2:]:
        copy.wait()


def prepare_kernel(
    valid_ref,
    table_ref,
    usable_ref,
    bias_ref,
    cells,
    table,
    mid,
    rows,
    sems,
):
    lat, lon, _ = coordinates()
    pairs = []
    above = pl.multiple_of(lax.rem(lat * ROWS + NLAT - ROWS, NLAT), ROWS)
    own = pl.multiple_of(lat * ROWS, ROWS)
    pairs.append((valid_ref.at[pl.ds(above, ROWS)], cells.at[pl.ds(0, ROWS)]))
    pairs.append((valid_ref.at[pl.ds(own, ROWS)], cells.at[pl.ds(ROWS, ROWS)]))
    copies = [
        pltpu.make_async_copy(source, target, sems.at[n])
        for n, (source, target) in enumerate(pairs)
    ]
    for copy in copies:
        copy.start()

    pick_one, pick_two = pick_step(), pick_entry()
    dims = (NLON, 128)
    wanted = lax.rem(iota((1, 128), 1) + lon * COLS + NLON - HALF, NLON)
    pick_cols = as_low(iota(dims, 0) == wanted)
    table[...] = jnp.zeros_like(table)
    table[:, 0:ENTRIES] = table_ref[...]
    spread = sum(against(part, pick_two) for part in exact_parts(table[...]))
    for b in range(WIN):
        mid[pl.ds(b, HEADS, stride=WIN), :] = spread[:, b * 128 : (b + 1) * 128]
    rows[...] = sum(against(part, pick_one) for part in exact_parts(mid[...]))
    for h in range(HEADS):
        for a in range(WIN):
            bias_ref[a * WIN : (a + 1) * WIN, h * CELLS : (h + 1) * CELLS] = rows[
                h * WIN : (h + 1) * WIN, a * CELLS : (a + 1) * CELLS
            ]

    for copy in copies:
        copy.wait()
    band = jnp.where(cells[HALF : HALF + ROWS, :] > 0, 1.0, 0.0).astype(bf16)
    line = dot(band, pick_cols)
    tall = jnp.concatenate(
        [jnp.broadcast_to(line[a : a + 1], (WIN, 128)) for a in range(WIN)], axis=0
    )
    row, lane = iota((CELLS, 128), 0), iota((CELLS, 128), 1)
    chosen = jnp.where((lane % WIN == row % WIN) & (lane < COLS), tall, 0.0).astype(bf16)
    window = as_low(iota((128, 128), 0) // WIN == iota((128, 128), 1))
    usable_ref[...] = dot(chosen, window)


def fields_kernel(
    out_in_ref,
    grad_in_ref,
    below_ref,
    side_ref,
    edge_ref,
    output_ref,
    grad_inputs_ref,
    wide,
    strip,
):
    for own_ref, out_ref, lanes in (
        (out_in_ref, output_ref, slice(0, CH)),
        (grad_in_ref, grad_inputs_ref, slice(CH, 2 * CH)),
    ):
        strip[0:16, :] = side_ref[:, lanes].astype(f32)
        strip[16:32, :] = edge_ref[:, lanes].astype(f32)
        for a in range(ROWS):
            if a < HALF:
                wide[0:COLS, :] = own_ref[a + HALF].astype(f32)
            else:
                wide[0:COLS, :] = below_ref[a - HALF, :, lanes].astype(f32)
            wide[COLS : COLS + HALF, :] = strip[a * HALF : (a + 1) * HALF, :]
            out_ref[a] = wide[HALF : HALF + COLS, :].astype(bf16)


def grads_kernel(
    mine_ref,
    other_ref,
    grad_qkv_ref,
    grad_proj_ref,
    grad_up_ref,
    grad_down_ref,
    gain_one_ref,
    shift_one_ref,
    gain_two_ref,
    shift_two_ref,
    table_ref,
):
    _, _, core = coordinates()
    first = core == 0

    def found(half, rows, lanes):
        mine, other = mine_ref[rows, lanes], other_ref[rows, lanes]
        return jnp.where(first == (half == 0), mine, other).astype(f32)

    def block(number):
        half, place = divmod(number, PER_HALF)
        return found(half, slice(0, CH), slice(place * CH, (place + 1) * CH))

    for k in range(MLP // CH):
        part = slice(k * CH, (k + 1) * CH)
        grad_down_ref[part, :] = block(k)
        grad_up_ref[:, part] = block(AT_UP + k)
    for k in range(3):
        grad_qkv_ref[:, k * CH : (k + 1) * CH] = block(AT_QKV + k)
    grad_proj_ref[...] = block(AT_PROJ)
    side = slice(PER_HALF * CH, WIDTH)
    small = jnp.concatenate(
        [found(0, slice(0, SMALL), side), found(0, slice(SMALL, 2 * SMALL), side)], axis=1
    )
    table_ref[...] = small[0:HEADS, 0:ENTRIES]
    gain_one_ref[...] = small[HEADS : HEADS + 1]
    shift_one_ref[...] = small[HEADS + 1 : HEADS + 2]
    gain_two_ref[...] = small[HEADS + 2 : HEADS + 3]
    shift_two_ref[...] = small[HEADS + 3 : HEADS + 4]


def in_vmem():
    return pl.BlockSpec(memory_space=pltpu.VMEM)


def shape(dims, dtype):
    return jax.ShapeDtypeStruct(dims, dtype)


def in_any():
    return pl.BlockSpec(memory_space=pl.ANY)


def run_cut(inputs, cotangent):
    return pl.pallas_call(
        cut_kernel,
        out_shape=(
            shape((HALF, COLS, 2 * CH), bf16),
            shape((16, 2 * CH), bf16),
            shape((16, 2 * CH), bf16),
        ),
        in_specs=[in_any()] * 2,
        out_specs=[in_vmem()] * 3,
        scratch_shapes=[
            pltpu.VMEM((2, ROWS, 16, CH), bf16),
            pltpu.VMEM((16, CH), f32),
            pltpu.VMEM((32, CH), f32),
            pltpu.SemaphoreType.DMA((4,)),
        ],
        compiler_params=pltpu.CompilerParams(vmem_limit_bytes=8 * 1024 * 1024),
        cost_estimate=pl.CostEstimate(flops=1000, bytes_accessed=1_000_000, transcendentals=0),
    )(inputs, cotangent)


def run_prepare(valid_cells, bias_table):
    return pl.pallas_call(
        prepare_kernel,
        out_shape=(shape((CELLS, 128), f32), shape((CELLS, PAIRS), f32)),
        in_specs=[in_any(), in_vmem()],
        out_specs=[in_vmem()] * 2,
        scratch_shapes=[
            pltpu.VMEM((2 * ROWS, NLON), jnp.int32),
            pltpu.VMEM((HEADS, CH), f32),
            pltpu.VMEM((CELLS, 128), f32),
            pltpu.VMEM((CELLS, PAIRS), f32),
            pltpu.SemaphoreType.DMA((2,)),
        ],
        compiler_params=pltpu.CompilerParams(vmem_limit_bytes=8 * 1024 * 1024),
        cost_estimate=pl.CostEstimate(
            flops=500_000_000, bytes_accessed=2_000_000, transcendentals=0
        ),
    )(valid_cells, bias_table)


def run_block(*operands):
    return pl.pallas_call(
        block_kernel,
        out_shape=(
            shape((ROWS, COLS, CH), bf16),
            shape((ROWS, COLS, CH), bf16),
            shape((HALF, COLS, 2 * CH), bf16),
            shape((16, 2 * CH), bf16),
            shape((16, 2 * CH), bf16),
            shape((CH, WIDTH), bf16),
            shape((CH, WIDTH), bf16),
        ),
        in_specs=[in_vmem()] * len(operands),
        out_specs=[in_vmem()] * 7,
        scratch_shapes=[
            pltpu.VMEM((COLS + 16, CH), f32),
            pltpu.VMEM((LOCAL, CH), f32),
            pltpu.VMEM((LOCAL, CH), bf16),
            pltpu.VMEM((LOCAL, CH), f32),
            pltpu.VMEM((LOCAL, CH), bf16),
            pltpu.VMEM((LOCAL, 3 * CH), bf16),
            pltpu.VMEM((LOCAL, PAIRS), f32),
            pltpu.VMEM((LOCAL, CH), bf16),
            pltpu.VMEM((LOCAL, CH), bf16),
            pltpu.VMEM((LOCAL, CH), f32),
            pltpu.VMEM((LOCAL, CH), f32),
            pltpu.VMEM((LOCAL, CH), bf16),
            pltpu.VMEM((LOCAL, CH), bf16),
            pltpu.VMEM((LOCAL, 3 * CH), bf16),
            pltpu.VMEM((PAIRS // 2, 128), bf16),
            pltpu.VMEM((CELLS, PAIRS), f32),
            pltpu.VMEM((CELLS, PAIRS), f32),
            pltpu.VMEM((CELLS, 128), f32),
            pltpu.VMEM((2, CH, WIDTH), bf16),
            pltpu.VMEM((LOCAL, PAIRS), f32),
            pltpu.VMEM((LOCAL, PAIRS), bf16),
            pltpu.VMEM((32, CH), f32),
        ],
        compiler_params=pltpu.CompilerParams(vmem_limit_bytes=32 * 1024 * 1024),
        cost_estimate=pl.CostEstimate(
            flops=4_000_000_000, bytes_accessed=8_000_000, transcendentals=2_000_000
        ),
    )(*operands)


def run_fields(*operands):
    return pl.pallas_call(
        fields_kernel,
        out_shape=(shape((ROWS, COLS, CH), bf16),) * 2,
        in_specs=[in_vmem()] * len(operands),
        out_specs=[in_vmem()] * 2,
        scratch_shapes=[pltpu.VMEM((COLS + 16, CH), f32), pltpu.VMEM((32, CH), f32)],
        compiler_params=pltpu.CompilerParams(vmem_limit_bytes=16 * 1024 * 1024),
        cost_estimate=pl.CostEstimate(flops=1_000_000, bytes_accessed=2_000_000, transcendentals=0),
    )(*operands)


def run_grads(mine, other):
    return pl.pallas_call(
        grads_kernel,
        out_shape=(
            shape((CH, 3 * CH), f32),
            shape((CH, CH), f32),
            shape((CH, MLP), f32),
            shape((MLP, CH), f32),
            shape((1, CH), f32),
            shape((1, CH), f32),
            shape((1, CH), f32),
            shape((1, CH), f32),
            shape((HEADS, ENTRIES), f32),
        ),
        in_specs=[in_vmem()] * 2,
        out_specs=[in_vmem()] * 9,
        compiler_params=pltpu.CompilerParams(vmem_limit_bytes=32 * 1024 * 1024),
        cost_estimate=pl.CostEstimate(flops=1_000_000, bytes_accessed=8_000_000, transcendentals=0),
    )(mine, other)


def total_over_chips(keep, give, beside):
    swap = [(0, 1), (1, 0)]
    pair = keep.astype(f32) + lax.ppermute(give, "c", swap).astype(f32)
    rows = CH // NEAR_SIZE
    pieces = pair.astype(bf16).reshape(NEAR_SIZE, rows, WIDTH)
    pieces = lax.all_to_all(pieces, NEAR, 0, 0, tiled=True)
    part = jnp.sum(pieces.astype(f32), axis=0).astype(bf16)
    copies = jnp.broadcast_to(part[None], (FAR_SIZE, rows, WIDTH))
    copies = lax.all_to_all(copies, FAR, 0, 0, tiled=True)
    part = jnp.sum(copies.astype(f32), axis=0).astype(bf16)
    copies = jnp.broadcast_to(part[None], (NEAR_SIZE, rows, WIDTH))
    mine = lax.all_to_all(copies, NEAR, 0, 0, tiled=True).reshape(CH, WIDTH)
    return mine, lax.ppermute(mine, "c", swap), beside


def per_device(
    inputs,
    cotangent,
    valid_cells,
    gain_one,
    shift_one,
    gain_two,
    shift_two,
    qkv_weight,
    proj_weight,
    up_weight,
    down_weight,
    bias_table,
):
    low_rows, top_last, low_last = run_cut(inputs, cotangent)
    above = moved(low_rows, 1, 0)
    beside = moved(top_last, 0, 1)
    corner = moved(low_last, 1, 1)
    usable, bias = run_prepare(valid_cells, bias_table)
    output, grad_inputs, below, side, edge, keep, give = run_block(
        inputs,
        cotangent,
        above,
        beside,
        corner,
        usable,
        gain_one.reshape(1, CH),
        shift_one.reshape(1, CH),
        gain_two.reshape(1, CH),
        shift_two.reshape(1, CH),
        qkv_weight,
        proj_weight,
        up_weight,
        down_weight,
        bias,
    )
    back = (moved(below, -1, 0), moved(side, 0, -1), moved(edge, -1, -1))
    mine, other, (below, side, edge) = total_over_chips(keep, give, back)
    grads = run_grads(mine, other)
    table, (below, side, edge) = lax.optimization_barrier((grads[-1], (below, side, edge)))
    fields = run_fields(output, grad_inputs, below, side, edge)
    grads = grads[:-1] + (table,)
    return fields + tuple(
        item.reshape(CH) if item.shape == (1, CH) else item for item in grads
    )


def solution(mesh):
    split = jax.sharding.Mesh(mesh.devices.reshape(SHAPE), EVERY)
    field = P(LAT, LON, None)
    return jax.shard_map(
        per_device,
        mesh=split,
        in_specs=(field, field) + (P(),) * 10,
        out_specs=(field, field) + (P(),) * 9,
        check_vma=False,
    )
```

```python
import math

import jax
import jax.numpy as jnp
from jax import lax
from jax.experimental import pallas as pl
from jax.experimental.pallas import tpu as pltpu
from jax.sharding import PartitionSpec as P

WIN = 8
CELLS = WIN * WIN
HALF = WIN // 2
CH = 256
HEADS = 8
HEAD_DIM = 32
MLP = 1024
NLAT = 128
NLON = 1024
ROWS = 8
COLS = 64
WINDOWS = COLS // WIN
LOCAL = ROWS * COLS
PAIRS = HEADS * CELLS
ENTRIES = (2 * WIN - 1) * (2 * WIN - 1)

EPSILON = 1e-05
ROOT_HALF = 0.7071067811865476
INV_ROOT_TAU = 0.3989422804014327
NEVER = -1e30

LAT = ("xl", "y", "c")
LON = ("xh", "zh", "zl")
EVERY = LAT + LON
NEAR = ("xl", "y", "xh", "zl")
FAR = "zh"
SHAPE = (2, 4, 2, 2, 4, 2)
SIDE = 16

BLOCKS = 12
AT_UP = 4
AT_QKV = 8
AT_PROJ = 11
SMALL = 16
NEAR_SIZE = 32
FAR_SIZE = 4
PER_HALF = BLOCKS // 2
WIDTH = PER_HALF * CH + 128

f32 = jnp.float32
bf16 = jnp.bfloat16


def moved(block, lat_step, lon_step):
    pairs = []
    for lat in range(SIDE):
        for lon in range(SIDE):
            target = ((lat + lat_step) % SIDE) * SIDE + (lon + lon_step) % SIDE
            pairs.append((lat * SIDE + lon, target))
    return lax.ppermute(block, EVERY, pairs)


def coordinates():
    lat = (lax.axis_index("xl") * 4 + lax.axis_index("y")) * 2 + lax.axis_index("c")
    return lat, lax.axis_index("xh") * 8 + lax.axis_index("zh") * 2 + lax.axis_index("zl"), (
        lax.axis_index("c")
    )


def dot(left, right):
    return jnp.dot(left, right, preferred_element_type=f32)


def across(left, right):
    return lax.dot_general(left, right, (((0,), (0,)), ((), ())), preferred_element_type=f32)


def against(left, right):
    return lax.dot_general(left, right, (((1,), (1,)), ((), ())), preferred_element_type=f32)


def split_dot(left, right):
    high = left.astype(bf16)
    low = (left - high.astype(f32)).astype(bf16)
    return dot(high, right) + dot(low, right)


def row_stats(values):
    centred = values - jnp.mean(values, axis=-1, keepdims=True)
    inv_std = lax.rsqrt(jnp.mean(centred * centred, axis=-1, keepdims=True) + EPSILON)
    return centred * inv_std, inv_std


def norm_back(upstream, normed, inv_std, gain_vec):
    scaled = upstream * gain_vec
    return inv_std * (
        scaled
        - jnp.mean(scaled, axis=-1, keepdims=True)
        - normed * jnp.mean(scaled * normed, axis=-1, keepdims=True)
    )


def block_kernel(
    inputs_ref,
    cotangent_ref,
    above_ref,
    beside_ref,
    corner_ref,
    cells_ref,
    gain_one_ref,
    shift_one_ref,
    gain_two_ref,
    shift_two_ref,
    qkv_weight_ref,
    proj_weight_ref,
    up_weight_ref,
    down_weight_ref,
    bias_ref,
    output_ref,
    grad_inputs_ref,
    below_ref,
    side_ref,
    edge_ref,
    keep_ref,
    give_ref,
    wide,
    tokens,
    upstream,
    hat_one,
    first_in,
    qkv,
    probs,
    mixed,
    second_in,
    total_out,
    total_back,
    d_resid,
    d_mixed,
    d_qkv,
    head_rows,
    score_total,
    score_rows,
    table_mid,
    packed,
    d_scores,
    low,
    strip,
    valid_ref,
    cells,
):
    scale = 1.0 / math.sqrt(LOCAL * SIDE * SIDE)

    def pack(block, values):
        half, place = divmod(block, PER_HALF)
        packed[half, :, place * CH : (place + 1) * CH] = (values * scale).astype(bf16)

    factor = HEAD_DIM**-0.5
    lat, lon, core = coordinates()
    fill_usable(cells_ref, valid_ref, cells, lat, lon)

    def assemble(own_ref, lanes, target):
        strip[0:16, :] = corner_ref[:, lanes].astype(f32)
        strip[16:32, :] = beside_ref[:, lanes].astype(f32)
        for a in range(ROWS):
            wide[16 - HALF : 16, :] = strip[a * HALF : (a + 1) * HALF, :]
            if a < HALF:
                wide[16 : 16 + COLS, :] = above_ref[a, :, lanes].astype(f32)
            else:
                wide[16 : 16 + COLS, :] = own_ref[a - HALF].astype(f32)
            line = wide[16 - HALF : 16 - HALF + COLS, :]
            for w in range(WINDOWS):
                target[w * CELLS + a * WIN : w * CELLS + (a + 1) * WIN, :] = line[
                    w * WIN : (w + 1) * WIN
                ].astype(target.dtype)

    assemble(inputs_ref, slice(0, CH), tokens)
    assemble(cotangent_ref, slice(CH, 2 * CH), total_back)
    upstream[...] = total_back[...].astype(bf16)

    lane_head = lax.broadcasted_iota(jnp.int32, (PAIRS // 2, 128), 1) // HEAD_DIM
    row_head = lax.broadcasted_iota(jnp.int32, (PAIRS // 2, 128), 0) // CELLS
    head_rows[...] = jnp.where(lane_head == row_head, 1.0, 0.0).astype(bf16)

    gain_one = gain_one_ref[...]
    normed, inv_one = row_stats(tokens[...])
    hat_one[...] = normed
    first = (normed * gain_one + shift_one_ref[...]).astype(bf16)
    first_in[...] = first
    qkv[...] = dot(first, qkv_weight_ref[...]).astype(bf16)

    halves = ((slice(0, 128), slice(0, PAIRS // 2)), (slice(128, CH), slice(PAIRS // 2, PAIRS)))
    lane_id = lax.broadcasted_iota(jnp.int32, (1, 128), 1)

    def spread(block):
        return [
            jnp.concatenate([block[:, lanes]] * (HEADS // 2), axis=0) * head_rows[...]
            for lanes, _ in halves
        ]

    def per_pair(block, spread_block):
        return jnp.concatenate(
            [against(block[:, lanes], half) for (lanes, _), half in zip(halves, spread_block)],
            axis=1,
        )

    def per_key(block, spread_block):
        return jnp.concatenate(
            [dot(block[:, pairs], half) for (_, pairs), half in zip(halves, spread_block)],
            axis=1,
        )

    def per_query(block, values):
        sides = []
        for lanes, pairs in halves:
            full = across(block[:, pairs], values[:, lanes])
            side = full[0:CELLS]
            for h in range(1, HEADS // 2):
                part = full[h * CELLS : (h + 1) * CELLS]
                side = jnp.where(lane_id >= h * HEAD_DIM, part, side)
            sides.append(side)
        return jnp.concatenate(sides, axis=1)

    key_id = lax.broadcasted_iota(jnp.int32, (CELLS, PAIRS), 0)
    query_id = lax.rem(lax.broadcasted_iota(jnp.int32, (CELLS, PAIRS), 1), CELLS)
    same_cell = key_id == query_id
    same_side = ((key_id < CELLS // 2) == (query_id < CELLS // 2)) | (lat > 0)

    def window(w):
        return slice(w * CELLS, (w + 1) * CELLS)

    for w in range(WINDOWS):
        rows = window(w)
        scores = per_pair(qkv[rows, CH : 2 * CH], spread(qkv[rows, 0:CH]))
        probs[rows, :] = scores * factor + bias_ref[...]
    for w in range(WINDOWS):
        rows = window(w)
        usable = jnp.broadcast_to(valid_ref[:, w : w + 1], (CELLS, PAIRS)) > 0.0
        scores = jnp.where((usable | same_cell) & same_side, probs[rows, :], NEVER)
        weights = jnp.exp(scores - jnp.max(scores, axis=0, keepdims=True))
        probs[rows, :] = weights * (1.0 / jnp.sum(weights, axis=0, keepdims=True))
    for w in range(WINDOWS):
        rows = window(w)
        values_in = qkv[rows, 2 * CH : 3 * CH]
        mixed[rows, :] = per_query(probs[rows, :].astype(bf16), values_in).astype(bf16)

    resid = (tokens[...] + dot(mixed[...], proj_weight_ref[...])).astype(bf16).astype(f32)
    hat_two, inv_two = row_stats(resid)
    gain_two = gain_two_ref[...]
    second_in[...] = (hat_two * gain_two + shift_two_ref[...]).astype(bf16)
    total_out[...] = resid
    total_back[...] = jnp.zeros_like(total_back)

    def feed(k):
        cols = slice(k * CH, (k + 1) * CH)
        up_part = up_weight_ref[:, cols]
        down_part = down_weight_ref[cols, :]
        second = second_in[...]
        grads = upstream[...]
        raised = dot(second, up_part)
        area = 0.5 * (1.0 + lax.erf(raised * ROOT_HALF))
        hidden = (raised * area).astype(bf16)
        slope = area + raised * jnp.exp(-0.5 * raised * raised) * INV_ROOT_TAU
        d_raised = (against(grads, down_part) * slope).astype(bf16)
        total_out[...] += dot(hidden, down_part)
        total_back[...] += against(d_raised, up_part)
        pack(k, across(hidden, grads))
        pack(AT_UP + k, across(second, d_raised))

    for k in range(MLP // CH):
        feed(k)

    def lay_out(values, out_ref, lanes):
        for a in range(ROWS):
            line = jnp.concatenate(
                [
                    values[w * CELLS + a * WIN : w * CELLS + (a + 1) * WIN]
                    for w in range(WINDOWS)
                ],
                axis=0,
            )
            strip[a * HALF : (a + 1) * HALF, :] = line[0:HALF]
            out_ref[a] = line.astype(bf16)
            if a < HALF:
                below_ref[a, :, lanes] = line.astype(bf16)
        edge_ref[:, lanes] = strip[0:16, :].astype(bf16)
        side_ref[:, lanes] = strip[16:32, :].astype(bf16)

    lay_out(total_out[...], output_ref, slice(0, CH))

    d_second = total_back[...]
    grad_gain_two = jnp.sum(d_second * hat_two, axis=0, keepdims=True)
    grad_shift_two = jnp.sum(d_second, axis=0, keepdims=True)
    back = norm_back(d_second, hat_two, inv_two, gain_two)
    d_low = (upstream[...].astype(f32) + back).astype(bf16)
    d_resid[...] = d_low
    pack(AT_PROJ, across(mixed[...], d_low))
    d_mixed[...] = against(d_low, proj_weight_ref[...]).astype(bf16)
    score_total[...] = jnp.zeros_like(score_total)

    for w in range(WINDOWS):
        rows = window(w)
        d_scores[rows, :] = per_pair(qkv[rows, 2 * CH : 3 * CH], spread(d_mixed[rows, :]))
    for w in range(WINDOWS):
        rows = window(w)
        share = probs[rows, :]
        d_share = d_scores[rows, :]
        back_scores = share * (d_share - jnp.sum(share * d_share, axis=0, keepdims=True))
        score_total[...] += back_scores
        low[rows, :] = back_scores.astype(bf16)
    for w in range(WINDOWS):
        rows = window(w)
        grads = spread(d_mixed[rows, :])
        queries = spread(qkv[rows, 0:CH])
        keys_in = qkv[rows, CH : 2 * CH]
        low_part = low[rows, :]
        d_qkv[rows, 0:CH] = (per_query(low_part, keys_in) * factor).astype(bf16)
        d_qkv[rows, CH : 2 * CH] = (per_key(low_part, queries) * factor).astype(bf16)
        d_qkv[rows, 2 * CH : 3 * CH] = per_key(probs[rows, :].astype(bf16), grads).astype(bf16)

    for part in range(3):
        lanes = slice(part * CH, (part + 1) * CH)
        pack(AT_QKV + part, across(first_in[...], d_qkv[:, lanes]))
    d_first = against(d_qkv[...], qkv_weight_ref[...])
    normed = hat_one[...]
    grad_gain_one = jnp.sum(d_first * normed, axis=0, keepdims=True)
    grad_shift_one = jnp.sum(d_first, axis=0, keepdims=True)
    back = norm_back(d_first, normed, inv_one, gain_one)
    lay_out(d_resid[...].astype(f32) + back, grad_inputs_ref, slice(CH, 2 * CH))

    for h in range(HEADS):
        for a in range(WIN):
            score_rows[h * WIN : (h + 1) * WIN, a * CELLS : (a + 1) * CELLS] = score_total[
                a * WIN : (a + 1) * WIN, h * CELLS : (h + 1) * CELLS
            ]
    table_mid[...] = split_dot(score_rows[...], pick_step())
    strips = [table_mid[pl.ds(b, HEADS, stride=WIN), :] for b in range(WIN)]
    table = split_dot(jnp.concatenate(strips, axis=1), pick_entry())
    small = jnp.concatenate(
        [table, grad_gain_one, grad_shift_one, grad_gain_two, grad_shift_two, jnp.zeros((4, CH), f32)],
        axis=0,
    )
    small = (small * scale).astype(bf16)
    side = slice(PER_HALF * CH, WIDTH)
    packed[0, 0:SMALL, side] = small[:, 0:128]
    packed[0, SMALL : 2 * SMALL, side] = small[:, 128:CH]
    packed[0, 2 * SMALL : CH, side] = jnp.zeros((CH - 2 * SMALL, 128), bf16)
    packed[1, :, side] = jnp.zeros((CH, 128), bf16)
    keep_ref[...] = packed[core]
    give_ref[...] = packed[1 - core]


def iota(dims, axis):
    return lax.broadcasted_iota(jnp.int32, dims, axis)


def as_low(choice):
    return jnp.where(choice, 1.0, 0.0).astype(bf16)


def pick_step():
    row = iota((PAIRS, 1), 0)
    wanted = (row // WIN % WIN - row // CELLS + WIN - 1) * WIN + row % WIN
    return as_low(wanted == iota((PAIRS, 128), 1))


def pick_entry():
    row = iota((WIN * 128, 1), 0)
    step = row // WIN % 16
    place = step * (2 * WIN - 1) + row % WIN - row // 128 + WIN - 1
    wanted = jnp.where(step < 2 * WIN - 1, place, -1)
    return as_low(wanted == iota((WIN * 128, CH), 1))


def exact_parts(values):
    high = values.astype(bf16)
    rest = values - high.astype(f32)
    mid = rest.astype(bf16)
    return high, mid, (rest - mid.astype(f32)).astype(bf16)


def cut_kernel(
    inputs_ref, cotangent_ref, rows_ref, cols_ref, edge_ref, grabbed, wide, strip, sems
):
    pairs = []
    for n, own_ref in enumerate((inputs_ref, cotangent_ref)):
        pairs.append((own_ref.at[:, pl.ds(COLS - 16, 16)], grabbed.at[n]))
    for n, own_ref in enumerate((inputs_ref, cotangent_ref)):
        pairs.append((own_ref.at[pl.ds(HALF, HALF)], rows_ref.at[:, :, pl.ds(n * CH, CH)]))
    copies = [
        pltpu.make_async_copy(source, target, sems.at[n])
        for n, (source, target) in enumerate(pairs)
    ]
    for copy in copies:
        copy.start()
    for n in range(2):
        copies[n].wait()
        lanes = slice(n * CH, (n + 1) * CH)
        for a in range(ROWS):
            wide[...] = grabbed[n, a].astype(f32)
            strip[a * HALF : (a + 1) * HALF, :] = wide[16 - HALF : 16, :]
        cols_ref[:, lanes] = strip[0:16, :].astype(bf16)
        edge_ref[:, lanes] = strip[16:32, :].astype(bf16)
    for copy in copies[2:]:
        copy.wait()


def bias_kernel(table_ref, bias_ref, table, mid, rows):
    pick_one, pick_two = pick_step(), pick_entry()
    table[...] = jnp.zeros_like(table)
    table[:, 0:ENTRIES] = table_ref[...]
    spread = sum(against(part, pick_two) for part in exact_parts(table[...]))
    for b in range(WIN):
        mid[pl.ds(b, HEADS, stride=WIN), :] = spread[:, b * 128 : (b + 1) * 128]
    rows[...] = sum(against(part, pick_one) for part in exact_parts(mid[...]))
    for h in range(HEADS):
        for a in range(WIN):
            bias_ref[a * WIN : (a + 1) * WIN, h * CELLS : (h + 1) * CELLS] = rows[
                h * WIN : (h + 1) * WIN, a * CELLS : (a + 1) * CELLS
            ]


def fill_usable(valid_ref, usable_ref, cells, lat, lon):
    above = pl.multiple_of(lax.rem(lat * ROWS + NLAT - ROWS, NLAT), ROWS)
    own = pl.multiple_of(lat * ROWS, ROWS)
    cells[0:ROWS, :] = valid_ref[pl.ds(above, ROWS), :]
    cells[ROWS : 2 * ROWS, :] = valid_ref[pl.ds(own, ROWS), :]
    wanted = lax.rem(iota((1, 128), 1) + lon * COLS + NLON - HALF, NLON)
    pick_cols = as_low(iota((NLON, 128), 0) == wanted)
    band = jnp.where(cells[HALF : HALF + ROWS, :] > 0, 1.0, 0.0).astype(bf16)
    line = dot(band, pick_cols)
    tall = jnp.concatenate(
        [jnp.broadcast_to(line[a : a + 1], (WIN, 128)) for a in range(WIN)], axis=0
    )
    row, lane = iota((CELLS, 128), 0), iota((CELLS, 128), 1)
    chosen = jnp.where((lane % WIN == row % WIN) & (lane < COLS), tall, 0.0).astype(bf16)
    window = as_low(iota((128, 128), 0) // WIN == iota((128, 128), 1))
    usable_ref[...] = dot(chosen, window)


def fields_kernel(
    out_in_ref,
    grad_in_ref,
    below_ref,
    side_ref,
    edge_ref,
    output_ref,
    grad_inputs_ref,
    wide,
    strip,
):
    for own_ref, out_ref, lanes in (
        (out_in_ref, output_ref, slice(0, CH)),
        (grad_in_ref, grad_inputs_ref, slice(CH, 2 * CH)),
    ):
        strip[0:16, :] = side_ref[:, lanes].astype(f32)
        strip[16:32, :] = edge_ref[:, lanes].astype(f32)
        for a in range(ROWS):
            if a < HALF:
                wide[0:COLS, :] = own_ref[a + HALF].astype(f32)
            else:
                wide[0:COLS, :] = below_ref[a - HALF, :, lanes].astype(f32)
            wide[COLS : COLS + HALF, :] = strip[a * HALF : (a + 1) * HALF, :]
            out_ref[a] = wide[HALF : HALF + COLS, :].astype(bf16)


def grads_kernel(
    mine_ref,
    other_ref,
    grad_qkv_ref,
    grad_proj_ref,
    grad_up_ref,
    grad_down_ref,
    gain_one_ref,
    shift_one_ref,
    gain_two_ref,
    shift_two_ref,
    table_ref,
):
    _, _, core = coordinates()
    first = core == 0

    def found(half, rows, lanes):
        mine, other = mine_ref[rows, lanes], other_ref[rows, lanes]
        return jnp.where(first == (half == 0), mine, other).astype(f32)

    def block(number):
        half, place = divmod(number, PER_HALF)
        return found(half, slice(0, CH), slice(place * CH, (place + 1) * CH))

    for k in range(MLP // CH):
        part = slice(k * CH, (k + 1) * CH)
        grad_down_ref[part, :] = block(k)
        grad_up_ref[:, part] = block(AT_UP + k)
    for k in range(3):
        grad_qkv_ref[:, k * CH : (k + 1) * CH] = block(AT_QKV + k)
    grad_proj_ref[...] = block(AT_PROJ)
    side = slice(PER_HALF * CH, WIDTH)
    small = jnp.concatenate(
        [found(0, slice(0, SMALL), side), found(0, slice(SMALL, 2 * SMALL), side)], axis=1
    )
    table_ref[...] = small[0:HEADS, 0:ENTRIES]
    gain_one_ref[...] = small[HEADS : HEADS + 1]
    shift_one_ref[...] = small[HEADS + 1 : HEADS + 2]
    gain_two_ref[...] = small[HEADS + 2 : HEADS + 3]
    shift_two_ref[...] = small[HEADS + 3 : HEADS + 4]


def in_vmem():
    return pl.BlockSpec(memory_space=pltpu.VMEM)


def shape(dims, dtype):
    return jax.ShapeDtypeStruct(dims, dtype)


def in_any():
    return pl.BlockSpec(memory_space=pl.ANY)


def run_cut(inputs, cotangent):
    return pl.pallas_call(
        cut_kernel,
        out_shape=(
            shape((HALF, COLS, 2 * CH), bf16),
            shape((16, 2 * CH), bf16),
            shape((16, 2 * CH), bf16),
        ),
        in_specs=[in_any()] * 2,
        out_specs=[in_vmem()] * 3,
        scratch_shapes=[
            pltpu.VMEM((2, ROWS, 16, CH), bf16),
            pltpu.VMEM((16, CH), f32),
            pltpu.VMEM((32, CH), f32),
            pltpu.SemaphoreType.DMA((4,)),
        ],
        compiler_params=pltpu.CompilerParams(vmem_limit_bytes=8 * 1024 * 1024),
        cost_estimate=pl.CostEstimate(flops=1000, bytes_accessed=1_000_000, transcendentals=0),
    )(inputs, cotangent)


def run_bias(bias_table):
    return pl.pallas_call(
        bias_kernel,
        out_shape=shape((CELLS, PAIRS), f32),
        in_specs=[in_vmem()],
        out_specs=in_vmem(),
        scratch_shapes=[
            pltpu.VMEM((HEADS, CH), f32),
            pltpu.VMEM((CELLS, 128), f32),
            pltpu.VMEM((CELLS, PAIRS), f32),
        ],
        compiler_params=pltpu.CompilerParams(vmem_limit_bytes=8 * 1024 * 1024),
        cost_estimate=pl.CostEstimate(
            flops=4_000_000_000, bytes_accessed=8_000_000, transcendentals=0
        ),
    )(bias_table)


def run_block(*operands):
    return pl.pallas_call(
        block_kernel,
        out_shape=(
            shape((ROWS, COLS, CH), bf16),
            shape((ROWS, COLS, CH), bf16),
            shape((HALF, COLS, 2 * CH), bf16),
            shape((16, 2 * CH), bf16),
            shape((16, 2 * CH), bf16),
            shape((CH, WIDTH), bf16),
            shape((CH, WIDTH), bf16),
        ),
        in_specs=[in_vmem()] * len(operands),
        out_specs=[in_vmem()] * 7,
        scratch_shapes=[
            pltpu.VMEM((COLS + 16, CH), f32),
            pltpu.VMEM((LOCAL, CH), f32),
            pltpu.VMEM((LOCAL, CH), bf16),
            pltpu.VMEM((LOCAL, CH), f32),
            pltpu.VMEM((LOCAL, CH), bf16),
            pltpu.VMEM((LOCAL, 3 * CH), bf16),
            pltpu.VMEM((LOCAL, PAIRS), f32),
            pltpu.VMEM((LOCAL, CH), bf16),
            pltpu.VMEM((LOCAL, CH), bf16),
            pltpu.VMEM((LOCAL, CH), f32),
            pltpu.VMEM((LOCAL, CH), f32),
            pltpu.VMEM((LOCAL, CH), bf16),
            pltpu.VMEM((LOCAL, CH), bf16),
            pltpu.VMEM((LOCAL, 3 * CH), bf16),
            pltpu.VMEM((PAIRS // 2, 128), bf16),
            pltpu.VMEM((CELLS, PAIRS), f32),
            pltpu.VMEM((CELLS, PAIRS), f32),
            pltpu.VMEM((CELLS, 128), f32),
            pltpu.VMEM((2, CH, WIDTH), bf16),
            pltpu.VMEM((LOCAL, PAIRS), f32),
            pltpu.VMEM((LOCAL, PAIRS), bf16),
            pltpu.VMEM((32, CH), f32),
            pltpu.VMEM((CELLS, 128), f32),
            pltpu.VMEM((2 * ROWS, NLON), jnp.int32),
        ],
        compiler_params=pltpu.CompilerParams(vmem_limit_bytes=32 * 1024 * 1024),
        cost_estimate=pl.CostEstimate(
            flops=4_000_000_000, bytes_accessed=8_000_000, transcendentals=2_000_000
        ),
    )(*operands)


def run_fields(*operands):
    return pl.pallas_call(
        fields_kernel,
        out_shape=(shape((ROWS, COLS, CH), bf16),) * 2,
        in_specs=[in_vmem()] * len(operands),
        out_specs=[in_vmem()] * 2,
        scratch_shapes=[pltpu.VMEM((COLS + 16, CH), f32), pltpu.VMEM((32, CH), f32)],
        compiler_params=pltpu.CompilerParams(vmem_limit_bytes=16 * 1024 * 1024),
        cost_estimate=pl.CostEstimate(flops=1_000_000, bytes_accessed=2_000_000, transcendentals=0),
    )(*operands)


def run_grads(mine, other):
    return pl.pallas_call(
        grads_kernel,
        out_shape=(
            shape((CH, 3 * CH), f32),
            shape((CH, CH), f32),
            shape((CH, MLP), f32),
            shape((MLP, CH), f32),
            shape((1, CH), f32),
            shape((1, CH), f32),
            shape((1, CH), f32),
            shape((1, CH), f32),
            shape((HEADS, ENTRIES), f32),
        ),
        in_specs=[in_vmem()] * 2,
        out_specs=[in_vmem()] * 9,
        compiler_params=pltpu.CompilerParams(vmem_limit_bytes=32 * 1024 * 1024),
        cost_estimate=pl.CostEstimate(flops=1_000_000, bytes_accessed=8_000_000, transcendentals=0),
    )(mine, other)


def total_over_chips(keep, give, beside):
    swap = [(0, 1), (1, 0)]
    pair = keep.astype(f32) + lax.ppermute(give, "c", swap).astype(f32)
    rows = CH // NEAR_SIZE
    pieces = pair.astype(bf16).reshape(NEAR_SIZE, rows, WIDTH)
    pieces = lax.all_to_all(pieces, NEAR, 0, 0, tiled=True)
    part = jnp.sum(pieces.astype(f32), axis=0).astype(bf16)
    copies = jnp.broadcast_to(part[None], (FAR_SIZE, rows, WIDTH))
    copies = lax.all_to_all(copies, FAR, 0, 0, tiled=True)
    part = jnp.sum(copies.astype(f32), axis=0).astype(bf16)
    copies = jnp.broadcast_to(part[None], (NEAR_SIZE, rows, WIDTH))
    mine = lax.all_to_all(copies, NEAR, 0, 0, tiled=True).reshape(CH, WIDTH)
    return mine, lax.ppermute(mine, "c", swap), beside


def per_device(
    inputs,
    cotangent,
    valid_cells,
    gain_one,
    shift_one,
    gain_two,
    shift_two,
    qkv_weight,
    proj_weight,
    up_weight,
    down_weight,
    bias_table,
):
    low_rows, top_last, low_last = run_cut(inputs, cotangent)
    above = moved(low_rows, 1, 0)
    beside = moved(top_last, 0, 1)
    corner = moved(low_last, 1, 1)
    output, grad_inputs, below, side, edge, keep, give = run_block(
        inputs,
        cotangent,
        above,
        beside,
        corner,
        valid_cells,
        gain_one.reshape(1, CH),
        shift_one.reshape(1, CH),
        gain_two.reshape(1, CH),
        shift_two.reshape(1, CH),
        qkv_weight,
        proj_weight,
        up_weight,
        down_weight,
        run_bias(bias_table),
    )
    back = (moved(below, -1, 0), moved(side, 0, -1), moved(edge, -1, -1))
    mine, other, (below, side, edge) = total_over_chips(keep, give, back)
    grads = run_grads(mine, other)
    table, (below, side, edge) = lax.optimization_barrier((grads[-1], (below, side, edge)))
    fields = run_fields(output, grad_inputs, below, side, edge)
    grads = grads[:-1] + (table,)
    return fields + tuple(
        item.reshape(CH) if item.shape == (1, CH) else item for item in grads
    )


def solution(mesh):
    split = jax.sharding.Mesh(mesh.devices.reshape(SHAPE), EVERY)
    field = P(LAT, LON, None)
    return jax.shard_map(
        per_device,
        mesh=split,
        in_specs=(field, field) + (P(),) * 10,
        out_specs=(field, field) + (P(),) * 9,
        check_vma=False,
    )
```
